256 devices in a mesh: lon: 16 (over z, core), lat: 8 (over x_hi, y), lev: 2 (over x_lo).
Axes of the slice: x: 4 (x_hi: 2, x_lo: 2; x = x_hi * 2 + x_lo), y: 4, z: 8, core: 2. Of those that a mesh axis runs over, the one named last changes fastest.
Arguments:
- fields: bfloat16 [2, 96, 768, 512], P('lev', 'lat', 'lon'), may hold values from -6 to 6
- cotangent: bfloat16 [2, 96, 768, 512], P('lev', 'lat', 'lon'), may hold values from -6 to 6
- land_mask: int32 [96, 768], P('lat', 'lon'), may hold values 0 or 1
- shift_offsets: int32 [2], replicated, may hold values from -40 to 39
- norm_gain: float32 [512], replicated, may hold values from 0.1 to 1.9
- w_qkv: bfloat16 [1536, 512], replicated, may hold values from -0.25 to 0.25
- w_proj: bfloat16 [512, 512], replicated, may hold values from -0.25 to 0.25
- rel_bias: float32 [8, 11, 23], replicated, may hold values from -260 to 260
Outputs:
- output: bfloat16 [2, 96, 768, 512], P('lev', 'lat', 'lon')
- grad_fields: bfloat16 [2, 96, 768, 512], P('lev', 'lat', 'lon')
- grad_qkv: float32 [1536, 512], P(('lon', 'lat', 'lev'))
- grad_proj: float32 [512, 512], P(('lon', 'lat', 'lev'))
- grad_bias: float32 [8, 11, 23], replicated
- grad_gain: float32 [512], replicated
The draws below stay inside these ranges and needn't reach their ends.
All inputs are finite; a program needn't handle non-finite values. No bound on the sum of `land_mask` on one device may be relied on, other than what follows from the above.
Results may differ from the reference program's by a relative error of at most 0.009.
Values may be sent and summed in bfloat16 or wider, within the bound.
A program may use at most 128 MiB of HBM per device.

```python
import jax
import jax.numpy as jnp
import numpy as np
from jax import lax

D = 512
HEADS = 8
WROWS = 6
WCOLS = 12
LEVELS = 2
NLAT = 96
NLON = 768


def draw_rel_bias(key, part):
    key = jax.random.fold_in(key, 7)
    table_shape = (HEADS, 2 * WROWS - 1, 2 * WCOLS - 1)
    return jnp.clip(2.0 * jax.random.normal(key, table_shape, jnp.float32), -12.0, 12.0)


def with_ends(array, own_key, low, high):
    spot = [jax.random.randint(jax.random.fold_in(own_key, axis), (), 0, length) for axis, length in enumerate(array.shape)]
    longest = array.shape.index(max(array.shape))
    next_to = spot[:longest] + [(spot[longest] + 1) % array.shape[longest]] + spot[longest + 1:]
    return array.at[tuple(spot)].set(low).at[tuple(next_to)].set(high)


def strengthened(array, own_key, source, target, blocks, factor):
    owner, partner = [(jnp.arange(array.shape[axis_at]) // (array.shape[axis_at] // blocks)).reshape([-1 if axis == axis_at else 1 for axis in range(array.ndim)]) for axis_at in (source, target)]
    chosen = jax.random.permutation(own_key, blocks)[partner]
    strong = (owner == chosen) | (owner == (partner + blocks // 2) % blocks)
    return jnp.where(strong, factor * array, array)


def shard_levels(rng, extent, shards, smallest, largest):
    gain = 1.0
    for axis_at, parts in shards:
        draws = jax.random.uniform(jax.random.fold_in(jax.random.fold_in(rng, 6), axis_at), (parts,), jnp.float32, smallest / len(shards), largest / len(shards))
        gain = gain * jnp.repeat(jnp.exp(draws), extent[axis_at] // parts).reshape((-1,) + (1,) * (len(extent) - 1 - axis_at))
    return gain


def centred(own_key, extent, width, limit, pieces=(), kind=jnp.bfloat16):
    loudness = shard_levels(own_key, extent, pieces, -0.22, 0.18) if pieces else 1.0
    values = jax.random.normal(own_key, extent, jnp.float32) * width * loudness
    return jnp.minimum(jnp.maximum(values, -limit), limit).astype(kind)


def noise_with(own_key, extent, scale, limit, shards, heavy, dtype=jnp.bfloat16):
    drawn = scale * jax.random.normal(own_key, extent, jnp.float32)
    if shards:
        drawn = drawn * shard_levels(own_key, extent, shards, -0.22, 0.18)
    return jnp.clip(strengthened(drawn, jax.random.fold_in(own_key, 3), *heavy), -limit, limit).astype(dtype)


def setup_inputs(seed: int = 0) -> dict:
    streams_of = jax.random.split(jax.random.key(seed), 9)
    fields = centred(streams_of[0], (LEVELS, NLAT, NLON, D), 1.0, 6.0, ((0, 2), (1, 8), (2, 16)))
    cotangent = noise_with(streams_of[1], (LEVELS, NLAT, NLON, D), 1.0, 6.0, ((0, 2), (1, 8), (2, 16)), (2, 3, 16, 2.0))
    land_mask = with_ends((jax.random.randint(streams_of[2], (NLAT, NLON), 0, 8) < 7).astype(jnp.int32), jax.random.fold_in(streams_of[2], 1), 0, 1)
    shift_offsets = jax.random.randint(streams_of[3], (2,), -40, 40).astype(jnp.int32)
    norm_gain = jnp.clip(1.0 + 0.18 * jax.random.normal(streams_of[4], (D,), jnp.float32), 0.1, 1.9)
    w_qkv = centred(streams_of[5], (3 * D, D), D ** -0.5, 0.25)
    w_proj = centred(streams_of[6], (D, D), D ** -0.5, 0.25)
    rel_bias = draw_rel_bias(jax.random.fold_in(streams_of[8], 71), 0)
    return {"fields": fields, "cotangent": cotangent, "land_mask": land_mask, "shift_offsets": shift_offsets, "norm_gain": norm_gain, "w_qkv": w_qkv, "w_proj": w_proj, "rel_bias": rel_bias}


EPSILON = 1e-05
NEG_FILL = 100.0

def offset_index():
    window_cells = WROWS * WCOLS
    cell_ids = np.arange(window_cells)
    row_place = cell_ids // WCOLS
    col_place = cell_ids % WCOLS
    lat_offset = row_place[:, None] - row_place[None, :] + WROWS - 1
    lon_offset = col_place[:, None] - col_place[None, :] + WCOLS - 1
    return (lat_offset, lon_offset)

def reference(fields, cotangent, land_mask, shift_offsets, norm_gain, w_qkv, w_proj, rel_bias):
    head_size = D // HEADS
    window_cells = WROWS * WCOLS
    scaling = head_size ** (-0.5)
    lat_shift = 1 + jnp.mod(shift_offsets[0], WROWS - 1)
    lon_shift = 1 + jnp.mod(shift_offsets[1], WCOLS - 1)
    lat_blocks = NLAT // WROWS + 1
    lon_blocks = NLON // WCOLS
    zero_index = jnp.zeros((), jnp.int32)
    lat_offset, lon_offset = offset_index()
    bias_full = rel_bias[:, lat_offset, lon_offset]

    def arrange(grid):
        trailing = grid.shape[3:]
        padding = [(0, 0), (WROWS, WROWS), (0, 0)] + [(0, 0)] * len(trailing)
        padded = jnp.pad(grid, padding)
        start_index = [zero_index, lat_shift.astype(jnp.int32), zero_index] + [zero_index] * len(trailing)
        region = lax.dynamic_slice(padded, start_index, (LEVELS, NLAT + WROWS, NLON) + trailing)
        region = jnp.roll(region, -lon_shift, axis=2)
        blocked = region.reshape((LEVELS, lat_blocks, WROWS, lon_blocks, WCOLS) + trailing)
        blocked = jnp.moveaxis(blocked, 3, 2)
        return blocked.reshape((LEVELS * lat_blocks, lon_blocks, window_cells) + trailing)

    def restore(stacked):
        trailing = stacked.shape[3:]
        blocked = stacked.reshape((LEVELS, lat_blocks, lon_blocks, WROWS, WCOLS) + trailing)
        blocked = jnp.moveaxis(blocked, 2, 3)
        region = blocked.reshape((LEVELS, lat_blocks * WROWS, NLON) + trailing)
        region = jnp.roll(region, lon_shift, axis=2)
        start_index = [zero_index, (WROWS - lat_shift).astype(jnp.int32), zero_index] + [zero_index] * len(trailing)
        return lax.dynamic_slice(region, start_index, (LEVELS, NLAT, NLON) + trailing)
    mask_grid = jnp.broadcast_to(land_mask, (LEVELS, NLAT, NLON)).astype(jnp.float32)
    inputs = (arrange(fields), arrange(cotangent), arrange(mask_grid))

    def one_row(carry, items):
        row_fields, row_grads, row_mask = items
        widened = row_fields.astype(jnp.float32).reshape(-1, D)
        center = lax.optimization_barrier(jnp.mean(widened, axis=-1, keepdims=True))
        spread = lax.optimization_barrier(jnp.mean(jnp.square(widened - center), axis=-1, keepdims=True))
        inverse = lax.rsqrt(spread + EPSILON)
        scaled = (widened - center) * inverse
        normed = (scaled * norm_gain).astype(jnp.bfloat16)
        qkv = jnp.dot(normed, w_qkv.T, preferred_element_type=jnp.float32).astype(jnp.bfloat16)
        qkv_wide = qkv.astype(jnp.float32).reshape(lon_blocks, window_cells, 3, HEADS, head_size)
        queries = qkv_wide[:, :, 0]
        keys_w = qkv_wide[:, :, 1]
        values_w = qkv_wide[:, :, 2]
        scores = jnp.einsum('wihd,wjhd->whij', queries, keys_w) * scaling + bias_full[None] + NEG_FILL * (row_mask[:, None, None, :] - 1.0)
        probs = jax.nn.softmax(scores, axis=-1)
        probs_back = lax.optimization_barrier(probs.astype(jnp.bfloat16)).astype(jnp.float32)
        mixed = jnp.einsum('whij,wjhd->wihd', probs_back, values_w).astype(jnp.bfloat16).reshape(-1, D)
        output = (widened + jnp.dot(mixed, w_proj.T, preferred_element_type=jnp.float32)).astype(jnp.bfloat16)
        grads_flat = row_grads.reshape(-1, D)
        grad_mixed = jnp.dot(grads_flat, w_proj, preferred_element_type=jnp.float32).astype(jnp.bfloat16)
        mixed_back = lax.optimization_barrier(grad_mixed).astype(jnp.float32).reshape(lon_blocks, window_cells, HEADS, head_size)
        proj_term = jnp.dot(grads_flat.T, mixed, preferred_element_type=jnp.float32)
        grad_values = jnp.einsum('whij,wihd->wjhd', probs_back, mixed_back)
        grad_probs = jnp.einsum('wihd,wjhd->whij', mixed_back, values_w)
        grad_scores = probs * (grad_probs - lax.optimization_barrier(jnp.sum(probs * grad_probs, axis=-1, keepdims=True)))
        bias_term = lax.optimization_barrier(jnp.sum(grad_scores, axis=0))
        scores_back = lax.optimization_barrier(grad_scores.astype(jnp.bfloat16)).astype(jnp.float32)
        grad_queries = jnp.einsum('whij,wjhd->wihd', scores_back, keys_w) * scaling
        grad_keys = jnp.einsum('whij,wihd->wjhd', scores_back, queries) * scaling
        grad_cells = jnp.stack([grad_queries, grad_keys, grad_values], axis=2).reshape(-1, 3 * D).astype(jnp.bfloat16)
        qkv_term = jnp.dot(grad_cells.T, normed, preferred_element_type=jnp.float32)
        grad_normed = jnp.dot(grad_cells, w_qkv, preferred_element_type=jnp.float32)
        gain_term = lax.optimization_barrier(jnp.sum(grad_normed * scaled, axis=0))
        grad_scaled = grad_normed * norm_gain
        grad_input = inverse * (grad_scaled - lax.optimization_barrier(jnp.mean(grad_scaled, axis=-1, keepdims=True)) - scaled * lax.optimization_barrier(jnp.mean(grad_scaled * scaled, axis=-1, keepdims=True)))
        grad_row = (grads_flat.astype(jnp.float32) + grad_input).astype(jnp.bfloat16)
        new_carry = (carry[0] + qkv_term, carry[1] + proj_term, carry[2] + bias_term, carry[3] + gain_term)
        return (new_carry, (output.reshape(lon_blocks, window_cells, D), grad_row.reshape(lon_blocks, window_cells, D)))
    start_carry = (jnp.zeros((3 * D, D), jnp.float32), jnp.zeros((D, D), jnp.float32), jnp.zeros((HEADS, window_cells, window_cells), jnp.float32), jnp.zeros((D,), jnp.float32))
    sums, rows_out = lax.scan(one_row, start_carry, inputs)
    grad_qkv, grad_proj, bias_total, grad_gain = sums
    output = restore(rows_out[0])
    grad_fields = restore(rows_out[1])
    grad_bias = jnp.zeros((HEADS, 2 * WROWS - 1, 2 * WCOLS - 1), jnp.float32).at[:, lat_offset, lon_offset].add(bias_total)
    return (output, grad_fields, grad_qkv, grad_proj, grad_bias, grad_gain)
```

```python
import jax
import jax.numpy as jnp
import numpy as np
from jax import lax
from jax.experimental import pallas as pl
from jax.experimental.pallas import tpu as pltpu
from jax.sharding import PartitionSpec as P

MESH = pl.DeviceIdType.MESH
WROWS = 6
WCOLS = 12
WCELLS = WROWS * WCOLS
WPAD = 80
EPSILON = 1e-05
NEG_FILL = 100.0
D = 512
HEADS = 8
ROWS = 12
COLS = 48
HALO_ROWS = 5
HALO_COLS = 16
EXT_ROWS = ROWS + 2 * HALO_ROWS
EXT_COLS = COLS + 2 * HALO_COLS
KBLOCKS = ROWS // WROWS + 1
MBLOCKS = COLS // WCOLS + 1
STRIP = MBLOCKS * WPAD
LAT = 8
LON = 16
LEV = 2
SMALL = 24
MB = 1024 * 1024
NT = (((1,), (1,)), ((), ()))
TN = (((0,), (0,)), ((), ()))


def mm(a, b):
    return jnp.dot(a, b, preferred_element_type=jnp.float32)


def mm_nt(a, b):
    return lax.dot_general(a, b, NT, preferred_element_type=jnp.float32)


def mm_tn(a, b):
    return lax.dot_general(a, b, TN, preferred_element_type=jnp.float32)


DIRECTIONS = [(dy, dx) for dy in (-1, 0, 1) for dx in (-1, 0, 1) if (dy, dx) != (0, 0)]
ROW_SRC = {1: (ROWS - HALO_ROWS, HALO_ROWS), 0: (0, ROWS), -1: (0, HALO_ROWS)}
ROW_DST = {1: 0, 0: HALO_ROWS, -1: HALO_ROWS + ROWS}
COL_SRC = {1: (COLS - HALO_COLS, HALO_COLS), 0: (0, COLS), -1: (0, HALO_COLS)}
COL_DST = {1: 0, 0: HALO_COLS, -1: HALO_COLS + COLS}


def halo_kernel(f_ref, c_ref, m_ref, fx_ref, cx_ref, mx_ref, send, recv, local):
    lon = lax.axis_index("lon")
    lat = lax.axis_index("lat")
    lev = lax.axis_index("lev")

    def neighbour(dy, dx):
        return (lax.rem(lon + dx + LON, LON), lax.rem(lat + dy + LAT, LAT), lev)

    barrier = pltpu.get_barrier_semaphore()
    for dy, dx in DIRECTIONS:
        pl.semaphore_signal(barrier, inc=1, device_id=neighbour(dy, dx), device_id_type=MESH)
    own = (pl.ds(HALO_ROWS, ROWS), pl.ds(HALO_COLS, COLS))
    locals_ = [
        pltpu.make_async_copy(f_ref, fx_ref.at[own[0], own[1]], local.at[0]),
        pltpu.make_async_copy(c_ref, cx_ref.at[own[0], own[1]], local.at[1]),
        pltpu.make_async_copy(m_ref, mx_ref.at[1, 1], local.at[2]),
    ]
    pl.semaphore_wait(barrier, len(DIRECTIONS))
    copies = []
    for n, (dy, dx) in enumerate(DIRECTIONS):
        rs, rn = ROW_SRC[dy]
        cs, cn = COL_SRC[dx]
        src = (pl.ds(rs, rn), pl.ds(cs, cn))
        dst = (pl.ds(ROW_DST[dy], rn), pl.ds(COL_DST[dx], cn))
        pairs = [
            (f_ref.at[src[0], src[1]], fx_ref.at[dst[0], dst[1]]),
            (c_ref.at[src[0], src[1]], cx_ref.at[dst[0], dst[1]]),
            (m_ref, mx_ref.at[1 - dy, 1 - dx]),
        ]
        for i, (a, b) in enumerate(pairs):
            copies.append(
                pltpu.make_async_remote_copy(
                    src_ref=a,
                    dst_ref=b,
                    send_sem=send.at[3 * n + i],
                    recv_sem=recv.at[3 * n + i],
                    device_id=neighbour(dy, dx),
                    device_id_type=MESH,
                )
            )
    for copy in copies:
        copy.start()
    for copy in locals_:
        copy.start()
    for copy in locals_:
        copy.wait()
    for copy in copies:
        copy.wait()


def halo(fields, cotangent, mask):
    any_spec = pl.BlockSpec(memory_space=pl.ANY)
    ext = jax.ShapeDtypeStruct((EXT_ROWS, EXT_COLS, D), jnp.bfloat16)
    return pl.pallas_call(
        halo_kernel,
        out_shape=(ext, ext, jax.ShapeDtypeStruct((3, 3, 16, 128), jnp.float32)),
        in_specs=[any_spec] * 3,
        out_specs=(any_spec,) * 3,
        scratch_shapes=[
            pltpu.SemaphoreType.DMA((24,)),
            pltpu.SemaphoreType.DMA((24,)),
            pltpu.SemaphoreType.DMA((3,)),
        ],
        compiler_params=pltpu.CompilerParams(collective_id=0, has_side_effects=True),
        name="halo_exchange",
    )(fields, cotangent, mask)


def cell_tables():
    cell = np.arange(STRIP)
    m, t = cell // WPAD, cell % WPAD
    a, b = t // WCOLS, t % WCOLS
    real = t < WCELLS
    info = np.zeros((STRIP, 4), np.int32)
    info[:, 0] = np.where(real, a * EXT_COLS + WCOLS * m + b, -100000)
    info[:, 1] = np.where(real, a, -1000)
    info[:, 2] = np.where(real, WCOLS * m + b, -1000)
    info[:, 3] = real
    lanes = np.zeros((8, STRIP), np.int32)
    lanes[0] = np.where(real, a * COLS, -100000)
    lanes[1] = np.where(real, WCOLS * m + b, -100000)
    win = np.zeros((8, WPAD), np.int32)
    t = np.arange(WPAD)
    win[0] = np.where(t < WCELLS, t // WCOLS, -1000)
    win[1] = np.where(t < WCELLS, t % WCOLS, -1000)
    perm = np.zeros((64, 64), np.float32)
    for o in range(8):
        for r in range(6):
            perm[8 * o + r, 6 * o + r] = 1
        for r in range(2):
            perm[8 * o + 6 + r, 48 + 2 * o + r] = 1
    return info, lanes, win, perm.astype(jnp.bfloat16)


def local_kernel(
    shift,
    fx_ref,
    cx_ref,
    mx_ref,
    gain_ref,
    wqkv_ref,
    wproj_ref,
    bias_ref,
    info_ref,
    lanes_ref,
    win_ref,
    perm_ref,
    out_ref,
    gf_ref,
    part_ref,
    g_ref,
    gg_ref,
    norm_s,
    mean_s,
    rstd_s,
    qkv_s,
    gm_s,
    key_s,
    mix_s,
    gc_s,
    mixo_s,
    gco_s,
):
    bf = jnp.bfloat16
    f32 = jnp.float32
    lat_shift = shift[0]
    lon_shift = shift[1]
    lat_base = shift[2]
    gain = gain_ref[...]
    g_ref[...] = jnp.zeros_like(g_ref)
    half = lax.broadcasted_iota(jnp.int32, (1, 128), 1) < 64
    lane4 = lax.broadcasted_iota(jnp.int32, (1, 256), 1)
    head_masks = [
        jnp.where((lane4 >= 64 * h) & (lane4 < 64 * h + 64), 1.0, 0.0).astype(bf) for h in range(4)
    ]

    def strip(k, carry):
        start = lat_shift - 1 + WROWS * k
        x = fx_ref[pl.ds(start, WROWS)].reshape(WROWS * EXT_COLS, D).astype(f32)
        mean = jnp.mean(x, axis=-1, keepdims=True)
        cen = x - mean
        var = jnp.mean(cen * cen, axis=-1, keepdims=True)
        rstd = lax.rsqrt(var + EPSILON)
        norm = (cen * rstd * gain).astype(bf)
        norm_s[pl.ds(WROWS * k, WROWS)] = norm.reshape(WROWS, EXT_COLS, D)
        mean_s[pl.ds(WROWS * k, WROWS)] = mean.reshape(WROWS, EXT_COLS, 1)
        rstd_s[pl.ds(WROWS * k, WROWS)] = rstd.reshape(WROWS, EXT_COLS, 1)
        acol = info_ref[:, 1:2]
        xcol = info_ref[:, 2:3] + (lon_shift + 4)
        grow = acol + (lat_shift - WROWS + WROWS * k + lat_base)
        valid = (grow >= 0) & (grow < LAT * ROWS)
        target = jnp.where(valid, info_ref[:, 0:1] + (lon_shift + 4), -1)
        lane = lax.broadcasted_iota(jnp.int32, (STRIP, WROWS * EXT_COLS), 1)
        pick = jnp.where(lane == target, 1.0, 0.0).astype(bf)
        nw = mm(pick, norm).astype(bf)
        cot = cx_ref[pl.ds(start, WROWS)].reshape(WROWS * EXT_COLS, D)
        cw = mm(pick, cot).astype(bf)
        qkv = mm_nt(nw, wqkv_ref[...]).astype(bf)
        qkv_s[:, : D] = qkv[:, : D] * jnp.asarray(0.125, bf)
        qkv_s[:, D:] = qkv[:, D:]
        gm_s[...] = mm(cw, wproj_ref[...]).astype(bf)
        lane = lax.broadcasted_iota(jnp.int32, (STRIP, 384), 1)
        mpick = (lane == xcol + 32) | (lane == xcol + 112) | (lane == xcol + 192)
        mpick = jnp.where(mpick, 1.0, 0.0).astype(bf)
        by_row = mm_nt(mpick, mx_ref[...].astype(bf))
        erow = acol + start
        flat = jnp.where(erow < 5, erow + 7, jnp.where(erow < 17, erow + 11, erow + 15))
        lane = lax.broadcasted_iota(jnp.int32, (STRIP, 48), 1)
        keep = jnp.sum(jnp.where((lane == flat) & valid, by_row, 0.0), axis=-1, keepdims=True)
        key_s[...] = jnp.where(info_ref[:, 3:4] > 0, NEG_FILL * (keep - 1.0), -1e30)
        win_row = win_ref[0:1, :] + (lat_shift - WROWS + WROWS * k)
        row_own = (win_row >= 0) & (win_row < ROWS)

        def window(m, c2):
            at = pl.multiple_of(m * WPAD, 16)
            sl = pl.ds(at, WPAD)
            key = key_s[sl, :]
            win_col = win_ref[1:2, :] + (lon_shift - WCOLS + WCOLS * m)
            own = jnp.where(row_own & (win_col >= 0) & (win_col < COLS), 1.0, 0.0)
            for q in range(2):
                lo = 256 * q
                qq = qkv_s[sl, lo : lo + 256]
                kq = qkv_s[sl, D + lo : D + lo + 256]
                vq = qkv_s[sl, 2 * D + lo : 2 * D + lo + 256]
                mq = gm_s[sl, lo : lo + 256]
                kst = jnp.concatenate([kq * h for h in head_masks], axis=0)
                vst = jnp.concatenate([vq * h for h in head_masks], axis=0)
                st = mm_nt(kst, qq).reshape(4, WPAD, WPAD)
                st = (st + bias_ref[4 * q : 4 * q + 4]) + key[None]
                top = jnp.max(st, axis=1, keepdims=True)
                ex = jnp.exp(st - top)
                pr = ex * (1.0 / jnp.sum(ex, axis=1, keepdims=True))
                prh = pr.astype(bf).reshape(4 * WPAD, WPAD)
                gp = mm_nt(vst, mq).reshape(4, WPAD, WPAD)
                pg = pr * gp
                ds = pr * (gp - jnp.sum(pg, axis=1, keepdims=True))
                g_ref[4 * q : 4 * q + 4] += ds * own[None]
                dsh = ds.astype(bf).reshape(4 * WPAD, WPAD)
                mix_s[sl, lo : lo + 256] = mm_tn(prh, vst).astype(bf)
                gc_s[sl, lo : lo + 256] = (mm_tn(dsh, kst) * 0.125).astype(bf)
                gk = mm(dsh, qq).reshape(4, WPAD, 256)
                gv = mm(prh, mq).reshape(4, WPAD, 256)
                for s, base in ((gk, D), (gv, 2 * D)):
                    for c in range(2):
                        lanes = slice(128 * c, 128 * c + 128)
                        both = jnp.where(half, s[2 * c, :, lanes], s[2 * c + 1, :, lanes])
                        gc_s[sl, base + lo + 128 * c : base + lo + 128 * c + 128] = both.astype(bf)
            return c2

        lax.fori_loop(0, MBLOCKS, window, 0)
        xl = lanes_ref[1:2, :] + (lon_shift - WCOLS)
        place = jnp.where((xl >= 0) & (xl < COLS), lanes_ref[0:1, :] + xl, -1)
        sub = lax.broadcasted_iota(jnp.int32, (WROWS * COLS, STRIP), 0)
        put = jnp.where(sub == place, 1.0, 0.0).astype(bf)
        mixo_s[pl.ds(WROWS * k, WROWS)] = mm(put, mix_s[...]).astype(bf).reshape(WROWS, COLS, D)
        gco_s[pl.ds(WROWS * k, WROWS)] = mm(put, gc_s[...]).astype(bf).reshape(WROWS, COLS, 3 * D)
        return carry

    lax.fori_loop(0, KBLOCKS, strip, 0)

    cells = ROWS * COLS
    first = pl.ds(WROWS - lat_shift, ROWS)
    own_cols = slice(HALO_COLS, HALO_COLS + COLS)
    own_rows = slice(HALO_ROWS, HALO_ROWS + ROWS)
    x = fx_ref[own_rows, own_cols, :].reshape(cells, D).astype(f32)
    cot = cx_ref[own_rows, own_cols, :].reshape(cells, D)
    norm = norm_s[first, own_cols, :].reshape(cells, D)
    mean = mean_s[first, own_cols, :].reshape(cells, 1)
    rstd = rstd_s[first, own_cols, :].reshape(cells, 1)
    mixo = mixo_s[first].reshape(cells, D)
    gco = gco_s[first].reshape(cells, 3 * D)
    out_ref[...] = (x + mm_nt(mixo, wproj_ref[...])).astype(bf).reshape(ROWS, COLS, D)
    gn = mm(gco, wqkv_ref[...])
    xhat = (x - mean) * rstd
    gg_ref[...] = jnp.sum(gn * xhat, axis=0, keepdims=True)
    gs = gn * gain
    gin = rstd * (
        gs
        - jnp.mean(gs, axis=-1, keepdims=True)
        - xhat * jnp.mean(gs * xhat, axis=-1, keepdims=True)
    )
    gf_ref[...] = (cot.astype(f32) + gin).astype(bf).reshape(ROWS, COLS, D)
    gq = mm_tn(gco, norm).astype(bf)
    gp = mm_tn(cot, mixo).astype(bf)
    for o in range(32):
        rows = jnp.concatenate([gq[48 * o : 48 * o + 48], gp[16 * o : 16 * o + 16]], axis=0)
        part_ref[64 * o : 64 * o + 64] = mm(perm_ref[...], rows).astype(bf)


def local(shift, fx, cx, mx, gain, w_qkv, w_proj, bias):
    info, lanes, win, perm = cell_tables()
    vmem = pl.BlockSpec(memory_space=pltpu.VMEM)
    smem = pl.BlockSpec(memory_space=pltpu.SMEM)
    tile = jax.ShapeDtypeStruct((ROWS, COLS, D), jnp.bfloat16)
    bf = jnp.bfloat16
    strip_rows = KBLOCKS * WROWS
    return pl.pallas_call(
        local_kernel,
        out_shape=(
            tile,
            tile,
            jax.ShapeDtypeStruct((2048, D), bf),
            jax.ShapeDtypeStruct((HEADS, WPAD, WPAD), jnp.float32),
            jax.ShapeDtypeStruct((1, D), jnp.float32),
        ),
        in_specs=[smem] + [vmem] * 11,
        out_specs=(vmem,) * 5,
        scratch_shapes=[
            pltpu.VMEM((strip_rows, EXT_COLS, D), bf),
            pltpu.VMEM((strip_rows, EXT_COLS, 1), jnp.float32),
            pltpu.VMEM((strip_rows, EXT_COLS, 1), jnp.float32),
            pltpu.VMEM((STRIP, 3 * D), bf),
            pltpu.VMEM((STRIP, D), bf),
            pltpu.VMEM((STRIP, 1), jnp.float32),
            pltpu.VMEM((STRIP, D), bf),
            pltpu.VMEM((STRIP, 3 * D), bf),
            pltpu.VMEM((strip_rows, COLS, D), bf),
            pltpu.VMEM((strip_rows, COLS, 3 * D), bf),
        ],
        compiler_params=pltpu.CompilerParams(vmem_limit_bytes=56 * MB),
        name="window_attention",
    )(
        shift, fx, cx, mx, gain, w_qkv, w_proj, bias,
        jnp.asarray(info), jnp.asarray(lanes), jnp.asarray(win), jnp.asarray(perm),
    )


PLANE = 16
ZED = 8


def reduce_kernel(
    part_ref, small_ref, rows_ref, total_ref,
    got_a, small_a, buf_b, got_b, small_b, buf_c, got_c, small_c, sum_a, sum_b,
    send_a, recv_a, send_b, recv_b, send_c, recv_c,
):
    bf = jnp.bfloat16
    f32 = jnp.float32
    lon = lax.axis_index("lon")
    lat = lax.axis_index("lat")
    lev = lax.axis_index("lev")
    zed = lon // 2
    core = lax.rem(lon, 2)
    plane = lat * 2 + lev
    sibling = (zed * 2 + (1 - core), lat, lev)

    def in_plane(p):
        return (lon, p // 2, lax.rem(p, 2))

    def along_z(z):
        return (z * 2 + core, lat, lev)

    barrier = pltpu.get_barrier_semaphore()
    pl.semaphore_signal(barrier, inc=1, device_id=sibling, device_id_type=MESH)
    for d in range(1, PLANE):
        p = lax.rem(plane + d, PLANE)
        pl.semaphore_signal(barrier, inc=1, device_id=in_plane(p), device_id_type=MESH)
    for d in range(1, ZED):
        z = lax.rem(zed + d, ZED)
        pl.semaphore_signal(barrier, inc=1, device_id=along_z(z), device_id_type=MESH)
    pl.semaphore_wait(barrier, 1 + PLANE - 1 + ZED - 1)

    def remote(src, dst, send, recv, to):
        return pltpu.make_async_remote_copy(
            src_ref=src, dst_ref=dst, send_sem=send, recv_sem=recv, device_id=to, device_id_type=MESH
        )

    copy_a = remote(part_ref.at[:, 1 - core], got_a, send_a.at[0], recv_a.at[0], sibling)
    copy_s = remote(small_ref, small_a, send_a.at[1], recv_a.at[1], sibling)
    copy_a.start()
    copy_s.start()
    copy_s.wait()
    sum_a[...] = small_ref[...] + small_a[...]
    copy_a.wait()
    for z in range(0, ZED, 2):
        lo = part_ref[z, core].astype(f32) + got_a[z].astype(f32)
        hi = part_ref[z + 1, core].astype(f32) + got_a[z + 1].astype(f32)
        both = jnp.concatenate(
            [lo.reshape(PLANE, 8, D), hi.reshape(PLANE, 8, D)], axis=1
        )
        buf_b[:, 8 * z : 8 * z + 16] = both.astype(bf)

    def copies_b(d):
        p = lax.rem(plane + d, PLANE)
        src = lax.rem(plane + (PLANE - d), PLANE)
        out = (
            remote(buf_b.at[p], got_b.at[d], send_b.at[2 * d], recv_b.at[2 * d], in_plane(p)),
            remote(sum_a, small_b.at[plane], send_b.at[2 * d + 1], recv_b.at[2 * d + 1], in_plane(p)),
        )
        return out, src

    for d in range(1, PLANE):
        for copy in copies_b(d)[0]:
            copy.start()
    acc = buf_b[plane].astype(f32)
    for d in range(1, PLANE):
        for copy in copies_b(d)[0]:
            copy.wait()
        acc = acc + got_b[d].astype(f32)
    small_b[plane] = sum_a[...]
    total = small_b[0]
    for p in range(1, PLANE):
        total = total + small_b[p]
    sum_b[...] = total

    for z in range(ZED):
        piece = acc[8 * z : 8 * z + 8]
        buf_c[z] = jnp.concatenate([piece[:, :256], piece[:, 256:]], axis=0).astype(bf)

    def copies_c(d):
        z = lax.rem(zed + d, ZED)
        return (
            remote(buf_c.at[z], got_c.at[d], send_c.at[2 * d], recv_c.at[2 * d], along_z(z)),
            remote(sum_b, small_c.at[zed], send_c.at[2 * d + 1], recv_c.at[2 * d + 1], along_z(z)),
        )

    for d in range(1, ZED):
        for copy in copies_c(d):
            copy.start()
    acc = buf_c[zed].astype(f32)
    for d in range(1, ZED):
        for copy in copies_c(d):
            copy.wait()
        acc = acc + got_c[d].astype(f32)
    rows_ref[:, :256] = acc[:8]
    rows_ref[:, 256:] = acc[8:]
    small_c[zed] = sum_b[...]
    total = small_c[0]
    for z in range(1, ZED):
        total = total + small_c[z]
    total_ref[...] = total


def reduce_all(part, small):
    vmem = pl.BlockSpec(memory_space=pltpu.VMEM)
    f32 = jnp.float32
    bf = jnp.bfloat16
    vm = pltpu.VMEM
    dma = pltpu.SemaphoreType.DMA
    return pl.pallas_call(
        reduce_kernel,
        out_shape=(
            jax.ShapeDtypeStruct((8, D), f32),
            jax.ShapeDtypeStruct((SMALL, 128), f32),
        ),
        in_specs=[vmem] * 2,
        out_specs=(vmem,) * 2,
        scratch_shapes=[
            vm((ZED, 128, D), bf),
            vm((SMALL, 128), f32),
            vm((PLANE, 64, D), bf),
            vm((PLANE, 64, D), bf),
            vm((PLANE, SMALL, 128), f32),
            vm((ZED, 16, 256), bf),
            vm((ZED, 16, 256), bf),
            vm((ZED, SMALL, 128), f32),
            vm((SMALL, 128), f32),
            vm((SMALL, 128), f32),
            dma((2,)),
            dma((2,)),
            dma((2 * PLANE,)),
            dma((2 * PLANE,)),
            dma((2 * ZED,)),
            dma((2 * ZED,)),
        ],
        compiler_params=pltpu.CompilerParams(
            collective_id=1, has_side_effects=True, vmem_limit_bytes=32 * MB
        ),
        name="reduce_gradients",
    )(part.reshape(ZED, 2, 128, D), small)


def offset_onehot():
    cell = np.arange(WPAD)
    a, b = cell // WCOLS, cell % WCOLS
    flat = (a[None, :] - a[:, None] + WROWS - 1) * (2 * WCOLS - 1) + (
        b[None, :] - b[:, None] + WCOLS - 1
    )
    real = (cell < WCELLS)[None, :] & (cell < WCELLS)[:, None]
    flat = np.where(real, flat, -1).astype(np.int32)
    entries = (2 * WROWS - 1) * (2 * WCOLS - 1)
    ids = lax.broadcasted_iota(jnp.int32, (entries, WPAD * WPAD), 0)
    return (ids == jnp.asarray(flat.reshape(1, -1))).astype(jnp.float32)


def on_device(fields, cotangent, land_mask, shift_offsets, norm_gain, w_qkv, w_proj, rel_bias):
    lat_shift = 1 + jnp.mod(shift_offsets[0], WROWS - 1)
    lon_shift = 1 + jnp.mod(shift_offsets[1], WCOLS - 1)
    shift = jnp.stack([lat_shift, lon_shift, lax.axis_index("lat") * ROWS]).astype(jnp.int32)
    mask = jnp.pad(land_mask.astype(jnp.float32), ((0, 4), (0, 80)))
    fx, cx, mx = halo(fields[0], cotangent[0], mask)
    mx = mx.transpose(0, 2, 1, 3).reshape(48, 384)
    onehot = offset_onehot()
    highest = lax.Precision.HIGHEST
    bias = jnp.dot(rel_bias.reshape(HEADS, -1), onehot, precision=highest)
    bias = bias.reshape(HEADS, WPAD, WPAD)
    out, gf, part, gsum, ggain = local(
        shift, fx, cx, mx, norm_gain.reshape(1, D), w_qkv, w_proj, bias
    )
    table = jnp.dot(gsum.reshape(HEADS, -1), onehot.T, precision=highest)
    small = jnp.concatenate([table.reshape(-1), ggain.reshape(-1)])
    entries = table.size
    small = jnp.pad(small, (0, SMALL * 128 - small.size)).reshape(SMALL, 128)
    rows, total = reduce_all(part, small)
    total = total.reshape(-1)
    return (
        out[None],
        gf[None],
        rows[:6],
        rows[6:],
        total[:entries].reshape(rel_bias.shape),
        total[entries : entries + D],
    )


def solution(mesh):
    return jax.shard_map(
        on_device,
        mesh=mesh,
        in_specs=(
            P("lev", "lat", "lon", None),
            P("lev", "lat", "lon", None),
            P("lat", "lon"),
            P(),
            P(),
            P(),
            P(),
            P(),
        ),
        out_specs=(
            P("lev", "lat", "lon", None),
            P("lev", "lat", "lon", None),
            P(("lon", "lat", "lev"), None),
            P(("lon", "lat", "lev"), None),
            P(),
            P(),
        ),
        check_vma=False,
    )
```

```python
import jax
import jax.numpy as jnp
import numpy as np
from jax import lax
from jax.experimental import pallas as pl
from jax.experimental.pallas import tpu as pltpu
from jax.sharding import PartitionSpec as P

MESH = pl.DeviceIdType.MESH
WROWS = 6
WCOLS = 12
WCELLS = WROWS * WCOLS
WPAD = 80
EPSILON = 1e-05
NEG_FILL = 100.0
D = 512
HEADS = 8
ROWS = 12
COLS = 48
HALO_ROWS = 5
HALO_COLS = 16
EXT_ROWS = ROWS + 2 * HALO_ROWS
EXT_COLS = COLS + 2 * HALO_COLS
KBLOCKS = ROWS // WROWS + 1
MBLOCKS = COLS // WCOLS + 1
STRIP = MBLOCKS * WPAD
LAT = 8
LON = 16
LEV = 2
SMALL = 24
MB = 1024 * 1024
NT = (((1,), (1,)), ((), ()))
TN = (((0,), (0,)), ((), ()))


def mm(a, b):
    return jnp.dot(a, b, preferred_element_type=jnp.float32)


def mm_nt(a, b):
    return lax.dot_general(a, b, NT, preferred_element_type=jnp.float32)


def mm_tn(a, b):
    return lax.dot_general(a, b, TN, preferred_element_type=jnp.float32)


UP, DOWN = 0, 1
LEFT, RIGHT = 0, 1
DIRECTIONS = [(dy, dx) for dy in (-1, 0, 1) for dx in (-1, 0, 1) if (dy, dx) != (0, 0)]
CENTRE = pl.ds(HALO_COLS, COLS)
FLAT = 256
OFFSETS = [(WROWS - 1) * (2 * WCOLS - 1) + WCOLS - 1 - (2 * WCOLS - 1) * (j // WCOLS) - j % WCOLS for j in range(WCELLS)]


def cell_tables():
    cell = np.arange(STRIP)
    m, t = cell // WPAD, cell % WPAD
    a, b = t // WCOLS, t % WCOLS
    real = t < WCELLS
    info = np.zeros((STRIP, 4), np.int32)
    info[:, 0] = np.where(real, a * EXT_COLS + WCOLS * m + b, -100000)
    info[:, 1] = np.where(real, a, -1000)
    info[:, 2] = np.where(real, WCOLS * m + b, -1000)
    info[:, 3] = real
    lanes = np.zeros((8, STRIP), np.int32)
    lanes[0] = np.where(real, a * COLS, -100000)
    lanes[1] = np.where(real, WCOLS * m + b, -100000)
    win = np.zeros((8, WPAD), np.int32)
    t = np.arange(WPAD)
    win[0] = np.where(t < WCELLS, t // WCOLS, -1000)
    win[1] = np.where(t < WCELLS, t % WCOLS, -1000)
    perm = np.zeros((64, 64), np.float32)
    for o in range(8):
        for r in range(6):
            perm[8 * o + r, 6 * o + r] = 1
        for r in range(2):
            perm[8 * o + 6 + r, 48 + 2 * o + r] = 1
    base = np.where(t < WCELLS, (2 * WCOLS - 1) * (t // WCOLS) + t % WCOLS, -1)
    obase = (np.arange(128)[:, None] == base[None, :]).astype(np.float32)
    return info, lanes, win, perm.astype(jnp.bfloat16), obase.astype(jnp.bfloat16)


def three_parts(x):
    hi = x.astype(jnp.bfloat16).astype(jnp.float32)
    rest = x - hi
    mid = rest.astype(jnp.bfloat16).astype(jnp.float32)
    return hi, mid, rest - mid


def normalized(x, gain):
    x = x.astype(jnp.float32)
    mean = jnp.mean(x, axis=-1, keepdims=True)
    cen = x - mean
    rstd = lax.rsqrt(jnp.mean(cen * cen, axis=-1, keepdims=True) + EPSILON)
    return mean, rstd, (cen * rstd * gain).astype(jnp.bfloat16)


def local_kernel(
    shift,
    f_ref,
    c_ref,
    m_ref,
    gain_ref,
    wqkv_ref,
    wproj_ref,
    rel_ref,
    info_ref,
    lanes_ref,
    win_ref,
    perm_ref,
    obase_ref,
    out_ref,
    gf_ref,
    part_ref,
    small_ref,
    tile_s,
    mx_s,
    vert_s,
    side_s,
    norm_s,
    cot_s,
    mean_s,
    rstd_s,
    roll_s,
    bias_s,
    g_s,
    z_s,
    qkv_s,
    gm_s,
    key_s,
    mix_s,
    gc_s,
    mixo_s,
    gco_s,
    send,
    recv,
):
    bf = jnp.bfloat16
    f32 = jnp.float32
    lon = lax.axis_index("lon")
    lat = lax.axis_index("lat")
    lev = lax.axis_index("lev")
    lat_shift = 1 + jnp.mod(shift[0], WROWS - 1)
    lon_shift = 1 + jnp.mod(shift[1], WCOLS - 1)
    lat_base = lat * ROWS
    has_above = lat > 0
    has_below = lat < LAT - 1
    true = lat >= 0

    def neighbour(dy, dx):
        return (lax.rem(lon + dx + LON, LON), lat + dy, lev)

    def exists(dy):
        return {-1: has_above, 0: true, 1: has_below}[dy]

    def remote(src, dst, n, to):
        return pltpu.make_async_remote_copy(
            src_ref=src, dst_ref=dst, send_sem=send.at[n], recv_sem=recv.at[n], device_id=to, device_id_type=MESH
        )

    barrier = pltpu.get_barrier_semaphore()
    for dy, dx in DIRECTIONS:

        @pl.when(exists(dy))
        def _(dy=dy, dx=dx):
            pl.semaphore_signal(barrier, inc=1, device_id=neighbour(dy, dx), device_id_type=MESH)

    tile_s[...] = jnp.zeros_like(tile_s)
    tile_s[:ROWS, :COLS] = m_ref[...].astype(f32)
    mx_s[1, 1] = tile_s[...]
    for absent, rows in ((lat == 0, UP), (lat == LAT - 1, DOWN)):

        @pl.when(absent)
        def _(rows=rows):
            vert_s[:, rows] = jnp.zeros_like(vert_s[:, rows])
            for block in range(3):
                mx_s[block, 2 * rows] = jnp.zeros((16, 128), f32)

    @pl.when(has_above & has_below)
    def _():
        pl.semaphore_wait(barrier, 8)

    @pl.when(~(has_above & has_below))
    def _():
        pl.semaphore_wait(barrier, 5)

    masks = []
    for n, (dy, dx) in enumerate(DIRECTIONS):
        copy = remote(tile_s, mx_s.at[1 - dx, 1 - dy], n, neighbour(dy, dx))
        masks.append((copy, exists(dy), exists(-dy)))
    vertical = []
    for way, dy, rows in ((DOWN, -1, pl.ds(0, HALO_ROWS)), (UP, 1, pl.ds(ROWS - HALO_ROWS, HALO_ROWS))):
        for i, src in enumerate((f_ref, c_ref)):
            copy = remote(src.at[rows], vert_s.at[i, way, :, CENTRE], 8 + 2 * way + i, neighbour(dy, 0))
            vertical.append((copy, exists(dy), exists(-dy)))
    for copy, sends, _ in masks + vertical:
        pl.when(sends)(copy.start)
    sides = []
    for s, dx, cols in ((LEFT, 1, pl.ds(COLS - HALO_COLS, HALO_COLS)), (RIGHT, -1, pl.ds(0, HALO_COLS))):
        for i, src in enumerate((f_ref, c_ref)):
            copy = remote(src.at[:, cols], side_s.at[i, s], 12 + 2 * s + i, neighbour(0, dx))
            copy.start()
            sides.append(copy)
    corners = []
    for way, there in ((UP, has_above), (DOWN, has_below)):
        for s, dx, cols, dst in (
            (LEFT, 1, pl.ds(COLS, HALO_COLS), pl.ds(0, HALO_COLS)),
            (RIGHT, -1, pl.ds(HALO_COLS, HALO_COLS), pl.ds(HALO_COLS + COLS, HALO_COLS)),
        ):
            for i in range(2):
                n = 16 + 4 * way + 2 * s + i
                copy = remote(vert_s.at[i, way, :, cols], vert_s.at[i, way, :, dst], n, neighbour(0, dx))
                corners.append((copy, there))

    gain = gain_ref[...]
    half = lax.broadcasted_iota(jnp.int32, (1, 128), 1) < 64
    lane4 = lax.broadcasted_iota(jnp.int32, (1, 256), 1)
    head_masks = [
        jnp.where((lane4 >= 64 * h) & (lane4 < 64 * h + 64), 1.0, 0.0).astype(bf) for h in range(4)
    ]
    g_s[...] = jnp.zeros_like(g_s)

    mean, rstd, norm = normalized(f_ref[...].reshape(ROWS * COLS, D), gain)
    mean_s[...] = mean
    rstd_s[...] = rstd
    own_rows = slice(HALO_ROWS, HALO_ROWS + ROWS)
    own_cols = slice(HALO_COLS, HALO_COLS + COLS)
    norm_s[own_rows, own_cols] = norm.reshape(ROWS, COLS, D)
    cot_s[own_rows, own_cols] = c_ref[...]

    rel3 = jnp.concatenate(three_parts(rel_ref[...]), axis=0)
    for j in range(WCELLS):
        roll_s[j] = pltpu.roll(rel3, (FLAT - OFFSETS[j]) % FLAT, 1)[:, :128]
    pairs = mm(roll_s[...].reshape(WCELLS * 24, 128).astype(bf), obase_ref[...])
    pairs = pairs.reshape(WCELLS, 24, WPAD)
    pairs = (pairs[:, 16:24] + pairs[:, 8:16]) + pairs[:, :8]
    bias_s[...] = jnp.zeros_like(bias_s)
    for j in range(WCELLS):
        bias_s[:, j, :] = pairs[j]

    for copy in sides:
        copy.wait()
    for s, cols in ((LEFT, slice(0, HALO_COLS)), (RIGHT, slice(HALO_COLS + COLS, EXT_COLS))):
        norm = normalized(side_s[0, s].reshape(ROWS * HALO_COLS, D), gain)[2]
        norm_s[own_rows, cols] = norm.reshape(ROWS, HALO_COLS, D)
        cot_s[own_rows, cols] = side_s[1, s]
    for copy, sends, receives in masks:
        pl.when(sends)(copy.wait_send)
        pl.when(receives)(copy.wait_recv)

    def strip(step, carry):
        k = lax.rem(step + 1, KBLOCKS)

        @pl.when(step == 1)
        def _():
            for copy, there in corners:
                pl.when(there)(copy.wait)
            for way, rows in ((UP, slice(0, HALO_ROWS)), (DOWN, slice(HALO_ROWS + ROWS, EXT_ROWS))):
                norm = normalized(vert_s[0, way].reshape(HALO_ROWS * EXT_COLS, D), gain)[2]
                norm_s[rows] = norm.reshape(HALO_ROWS, EXT_COLS, D)
                cot_s[rows] = vert_s[1, way]

        start = lat_shift - 1 + WROWS * k
        acol = info_ref[:, 1:2]
        xcol = info_ref[:, 2:3] + (lon_shift + 4)
        grow = acol + (lat_shift - WROWS + WROWS * k + lat_base)
        valid = (grow >= 0) & (grow < LAT * ROWS)
        target = jnp.where(valid, info_ref[:, 0:1] + (lon_shift + 4), -1)
        lane = lax.broadcasted_iota(jnp.int32, (STRIP, WROWS * EXT_COLS), 1)
        pick = jnp.where(lane == target, 1.0, 0.0).astype(bf)
        norm = norm_s[pl.ds(start, WROWS)].reshape(WROWS * EXT_COLS, D)
        nw = mm(pick, norm).astype(bf)
        cot = cot_s[pl.ds(start, WROWS)].reshape(WROWS * EXT_COLS, D)
        cw = mm(pick, cot).astype(bf)
        qkv = mm_nt(nw, wqkv_ref[...]).astype(bf)
        qkv_s[:, :D] = qkv[:, :D] * jnp.asarray(0.125, bf)
        qkv_s[:, D:] = qkv[:, D:]
        gm_s[...] = mm(cw, wproj_ref[...]).astype(bf)
        lane = lax.broadcasted_iota(jnp.int32, (STRIP, 128), 1)
        by_row = 0.0
        for block, offset in enumerate((32, -16, -64)):
            mpick = jnp.where(lane == xcol + offset, 1.0, 0.0).astype(bf)
            by_row = by_row + mm_nt(mpick, mx_s[block].reshape(48, 128).astype(bf))
        erow = acol + start
        flat = jnp.where(erow < 5, erow + 7, jnp.where(erow < 17, erow + 11, erow + 15))
        lane = lax.broadcasted_iota(jnp.int32, (STRIP, 48), 1)
        keep = jnp.sum(jnp.where((lane == flat) & valid, by_row, 0.0), axis=-1, keepdims=True)
        key_s[...] = jnp.where(info_ref[:, 3:4] > 0, NEG_FILL * (keep - 1.0), -1e30)
        win_row = win_ref[0:1, :] + (lat_shift - WROWS + WROWS * k)
        row_own = (win_row >= 0) & (win_row < ROWS)

        def window(m, c2):
            @pl.when((step == 0) & (m == 2))
            def _():
                for copy, sends, receives in vertical:
                    pl.when(receives)(copy.wait_recv)
                for copy, there in corners:
                    pl.when(there)(copy.start)
                for copy, sends, receives in vertical:
                    pl.when(sends)(copy.wait_send)

            at = pl.multiple_of(m * WPAD, 16)
            sl = pl.ds(at, WPAD)
            key = key_s[sl, :]
            win_col = win_ref[1:2, :] + (lon_shift - WCOLS + WCOLS * m)
            own = jnp.where(row_own & (win_col >= 0) & (win_col < COLS), 1.0, 0.0)
            for q in range(2):
                lo = 256 * q
                qq = qkv_s[sl, lo : lo + 256]
                kq = qkv_s[sl, D + lo : D + lo + 256]
                vq = qkv_s[sl, 2 * D + lo : 2 * D + lo + 256]
                mq = gm_s[sl, lo : lo + 256]
                kst = jnp.concatenate([kq * h for h in head_masks], axis=0)
                vst = jnp.concatenate([vq * h for h in head_masks], axis=0)
                st = mm_nt(kst, qq).reshape(4, WPAD, WPAD)
                st = (st + bias_s[4 * q : 4 * q + 4]) + key[None]
                top = jnp.max(st, axis=1, keepdims=True)
                ex = jnp.exp(st - top)
                pr = ex * (1.0 / jnp.sum(ex, axis=1, keepdims=True))
                prh = pr.astype(bf).reshape(4 * WPAD, WPAD)
                gp = mm_nt(vst, mq).reshape(4, WPAD, WPAD)
                pg = pr * gp
                ds = pr * (gp - jnp.sum(pg, axis=1, keepdims=True))
                g_s[4 * q : 4 * q + 4] += ds * own[None]
                dsh = ds.astype(bf).reshape(4 * WPAD, WPAD)
                mix_s[sl, lo : lo + 256] = mm_tn(prh, vst).astype(bf)
                gc_s[sl, lo : lo + 256] = (mm_tn(dsh, kst) * 0.125).astype(bf)
                gk = mm(dsh, qq).reshape(4, WPAD, 256)
                gv = mm(prh, mq).reshape(4, WPAD, 256)
                for s, base in ((gk, D), (gv, 2 * D)):
                    for c in range(2):
                        lanes = slice(128 * c, 128 * c + 128)
                        both = jnp.where(half, s[2 * c, :, lanes], s[2 * c + 1, :, lanes])
                        gc_s[sl, base + lo + 128 * c : base + lo + 128 * c + 128] = both.astype(bf)
            return c2

        lax.fori_loop(0, MBLOCKS, window, 0)
        xl = lanes_ref[1:2, :] + (lon_shift - WCOLS)
        place = jnp.where((xl >= 0) & (xl < COLS), lanes_ref[0:1, :] + xl, -1)
        sub = lax.broadcasted_iota(jnp.int32, (WROWS * COLS, STRIP), 0)
        put = jnp.where(sub == place, 1.0, 0.0).astype(bf)
        mixo_s[pl.ds(WROWS * k, WROWS)] = mm(put, mix_s[...]).astype(bf).reshape(WROWS, COLS, D)
        gco_s[pl.ds(WROWS * k, WROWS)] = mm(put, gc_s[...]).astype(bf).reshape(WROWS, COLS, 3 * D)
        return carry

    lax.fori_loop(0, KBLOCKS, strip, 0)

    cells = ROWS * COLS
    first = pl.ds(WROWS - lat_shift, ROWS)
    x = f_ref[...].reshape(cells, D).astype(f32)
    cot = c_ref[...].reshape(cells, D)
    norm = norm_s[own_rows, own_cols].reshape(cells, D)
    mean = mean_s[...]
    rstd = rstd_s[...]
    mixo = mixo_s[first].reshape(cells, D)
    gco = gco_s[first].reshape(cells, 3 * D)
    out_ref[...] = (x + mm_nt(mixo, wproj_ref[...])).astype(bf).reshape(ROWS, COLS, D)
    gn = mm(gco, wqkv_ref[...])
    xhat = (x - mean) * rstd
    gg = jnp.sum(gn * xhat, axis=0, keepdims=True)
    gs = gn * gain
    gin = rstd * (
        gs
        - jnp.mean(gs, axis=-1, keepdims=True)
        - xhat * jnp.mean(gs * xhat, axis=-1, keepdims=True)
    )
    gf_ref[...] = (cot.astype(f32) + gin).astype(bf).reshape(ROWS, COLS, D)
    gq = mm_tn(gco, norm).astype(bf)
    gp = mm_tn(cot, mixo).astype(bf)
    for o in range(32):
        rows = jnp.concatenate([gq[48 * o : 48 * o + 48], gp[16 * o : 16 * o + 16]], axis=0)
        part_ref[64 * o : 64 * o + 64] = mm(perm_ref[...], rows).astype(bf)

    small_ref[...] = jnp.zeros_like(small_ref)
    parts = three_parts(g_s[...].reshape(HEADS * WPAD, WPAD))
    z = mm_nt(parts[2].astype(bf), obase_ref[...]) + mm_nt(parts[1].astype(bf), obase_ref[...])
    z = z + mm_nt(parts[0].astype(bf), obase_ref[...])
    z_s[...] = z.reshape(HEADS, WPAD, 128)
    zero = jnp.zeros((HEADS, 128), f32)
    table = jnp.zeros((HEADS, FLAT), f32)
    for j in range(WCELLS):
        wide = jnp.concatenate([z_s[:, j, :], zero], axis=1)
        table = table + pltpu.roll(wide, OFFSETS[j], 1)
    small_ref[0:8, :] = table[:, :128]
    small_ref[8:16, :] = table[:, 128:]
    for i in range(4):
        small_ref[16 + i : 17 + i, :] = gg[:, 128 * i : 128 * i + 128]


def local(shift, fields, cotangent, mask, gain, w_qkv, w_proj, rel):
    info, lanes, win, perm, obase = cell_tables()
    vmem = pl.BlockSpec(memory_space=pltpu.VMEM)
    smem = pl.BlockSpec(memory_space=pltpu.SMEM)
    tile = jax.ShapeDtypeStruct((ROWS, COLS, D), jnp.bfloat16)
    bf = jnp.bfloat16
    f32 = jnp.float32
    vm = pltpu.VMEM
    dma = pltpu.SemaphoreType.DMA
    strip_rows = KBLOCKS * WROWS
    return pl.pallas_call(
        local_kernel,
        out_shape=(
            tile,
            tile,
            jax.ShapeDtypeStruct((2048, D), bf),
            jax.ShapeDtypeStruct((SMALL, 128), f32),
        ),
        in_specs=[smem] + [vmem] * 12,
        out_specs=(vmem,) * 4,
        scratch_shapes=[
            vm((16, 128), f32),
            vm((3, 3, 16, 128), f32),
            vm((2, 2, HALO_ROWS, EXT_COLS, D), bf),
            vm((2, 2, ROWS, HALO_COLS, D), bf),
            vm((EXT_ROWS, EXT_COLS, D), bf),
            vm((EXT_ROWS, EXT_COLS, D), bf),
            vm((ROWS * COLS, 1), f32),
            vm((ROWS * COLS, 1), f32),
            vm((WCELLS, 24, 128), f32),
            vm((HEADS, WPAD, WPAD), f32),
            vm((HEADS, WPAD, WPAD), f32),
            vm((HEADS, WPAD, 128), f32),
            vm((STRIP, 3 * D), bf),
            vm((STRIP, D), bf),
            vm((STRIP, 1), f32),
            vm((STRIP, D), bf),
            vm((STRIP, 3 * D), bf),
            vm((strip_rows, COLS, D), bf),
            vm((strip_rows, COLS, 3 * D), bf),
            dma((24,)),
            dma((24,)),
        ],
        compiler_params=pltpu.CompilerParams(
            collective_id=0, has_side_effects=True, vmem_limit_bytes=56 * MB
        ),
        name="window_attention",
    )(
        shift, fields, cotangent, mask, gain, w_qkv, w_proj, rel,
        jnp.asarray(info), jnp.asarray(lanes), jnp.asarray(win), jnp.asarray(perm), jnp.asarray(obase),
    )


PLANE = 16
ZED = 8


def reduce_kernel(
    part_ref, small_ref, rows_ref, total_ref,
    got_a, small_a, buf_b, got_b, small_b, buf_c, got_c, small_c, sum_a, sum_b,
    send_a, recv_a, send_b, recv_b, send_c, recv_c,
):
    bf = jnp.bfloat16
    f32 = jnp.float32
    lon = lax.axis_index("lon")
    lat = lax.axis_index("lat")
    lev = lax.axis_index("lev")
    zed = lon // 2
    core = lax.rem(lon, 2)
    plane = lat * 2 + lev
    sibling = (zed * 2 + (1 - core), lat, lev)

    def in_plane(p):
        return (lon, p // 2, lax.rem(p, 2))

    def along_z(z):
        return (z * 2 + core, lat, lev)

    barrier = pltpu.get_barrier_semaphore()
    pl.semaphore_signal(barrier, inc=1, device_id=sibling, device_id_type=MESH)
    for d in range(1, PLANE):
        p = lax.rem(plane + d, PLANE)
        pl.semaphore_signal(barrier, inc=1, device_id=in_plane(p), device_id_type=MESH)
    for d in range(1, ZED):
        z = lax.rem(zed + d, ZED)
        pl.semaphore_signal(barrier, inc=1, device_id=along_z(z), device_id_type=MESH)
    pl.semaphore_wait(barrier, 1 + PLANE - 1 + ZED - 1)

    def remote(src, dst, send, recv, to):
        return pltpu.make_async_remote_copy(
            src_ref=src, dst_ref=dst, send_sem=send, recv_sem=recv, device_id=to, device_id_type=MESH
        )

    copy_a = remote(part_ref.at[:, 1 - core], got_a, send_a.at[0], recv_a.at[0], sibling)
    copy_s = remote(small_ref, small_a, send_a.at[1], recv_a.at[1], sibling)
    copy_a.start()
    copy_s.start()
    copy_s.wait()
    sum_a[...] = small_ref[...] + small_a[...]
    copy_a.wait()
    for z in range(0, ZED, 2):
        lo = part_ref[z, core].astype(f32) + got_a[z].astype(f32)
        hi = part_ref[z + 1, core].astype(f32) + got_a[z + 1].astype(f32)
        both = jnp.concatenate(
            [lo.reshape(PLANE, 8, D), hi.reshape(PLANE, 8, D)], axis=1
        )
        buf_b[:, 8 * z : 8 * z + 16] = both.astype(bf)

    def copies_b(d):
        p = lax.rem(plane + d, PLANE)
        src = lax.rem(plane + (PLANE - d), PLANE)
        out = (
            remote(buf_b.at[p], got_b.at[d], send_b.at[2 * d], recv_b.at[2 * d], in_plane(p)),
            remote(sum_a, small_b.at[plane], send_b.at[2 * d + 1], recv_b.at[2 * d + 1], in_plane(p)),
        )
        return out, src

    for d in range(1, PLANE):
        for copy in copies_b(d)[0]:
            copy.start()
    acc = buf_b[plane].astype(f32)
    for d in range(1, PLANE):
        for copy in copies_b(d)[0]:
            copy.wait()
        acc = acc + got_b[d].astype(f32)
    small_b[plane] = sum_a[...]
    total = small_b[0]
    for p in range(1, PLANE):
        total = total + small_b[p]
    sum_b[...] = total

    for z in range(ZED):
        piece = acc[8 * z : 8 * z + 8]
        buf_c[z] = jnp.concatenate([piece[:, :256], piece[:, 256:]], axis=0).astype(bf)

    def copies_c(d):
        z = lax.rem(zed + d, ZED)
        return (
            remote(buf_c.at[z], got_c.at[d], send_c.at[2 * d], recv_c.at[2 * d], along_z(z)),
            remote(sum_b, small_c.at[zed], send_c.at[2 * d + 1], recv_c.at[2 * d + 1], along_z(z)),
        )

    for d in range(1, ZED):
        for copy in copies_c(d):
            copy.start()
    acc = buf_c[zed].astype(f32)
    for d in range(1, ZED):
        for copy in copies_c(d):
            copy.wait()
        acc = acc + got_c[d].astype(f32)
    rows_ref[:, :256] = acc[:8]
    rows_ref[:, 256:] = acc[8:]
    small_c[zed] = sum_b[...]
    total = small_c[0]
    for z in range(1, ZED):
        total = total + small_c[z]
    total_ref[...] = total


def reduce_all(part, small):
    vmem = pl.BlockSpec(memory_space=pltpu.VMEM)
    f32 = jnp.float32
    bf = jnp.bfloat16
    vm = pltpu.VMEM
    dma = pltpu.SemaphoreType.DMA
    return pl.pallas_call(
        reduce_kernel,
        out_shape=(
            jax.ShapeDtypeStruct((8, D), f32),
            jax.ShapeDtypeStruct((SMALL, 128), f32),
        ),
        in_specs=[vmem] * 2,
        out_specs=(vmem,) * 2,
        scratch_shapes=[
            vm((ZED, 128, D), bf),
            vm((SMALL, 128), f32),
            vm((PLANE, 64, D), bf),
            vm((PLANE, 64, D), bf),
            vm((PLANE, SMALL, 128), f32),
            vm((ZED, 16, 256), bf),
            vm((ZED, 16, 256), bf),
            vm((ZED, SMALL, 128), f32),
            vm((SMALL, 128), f32),
            vm((SMALL, 128), f32),
            dma((2,)),
            dma((2,)),
            dma((2 * PLANE,)),
            dma((2 * PLANE,)),
            dma((2 * ZED,)),
            dma((2 * ZED,)),
        ],
        compiler_params=pltpu.CompilerParams(
            collective_id=1, has_side_effects=True, vmem_limit_bytes=32 * MB
        ),
        name="reduce_gradients",
    )(part.reshape(ZED, 2, 128, D), small)


def on_device(fields, cotangent, land_mask, shift_offsets, norm_gain, w_qkv, w_proj, rel_bias):
    entries = rel_bias.shape[1] * rel_bias.shape[2]
    rel = jnp.pad(rel_bias.reshape(HEADS, entries), ((0, 0), (0, FLAT - entries)))
    out, gf, part, small = local(
        shift_offsets, fields[0], cotangent[0], land_mask, norm_gain.reshape(1, D), w_qkv, w_proj, rel
    )
    rows, total = reduce_all(part, small)
    table = jnp.concatenate([total[0:8], total[8:16]], axis=1)[:, :entries]
    return (
        out[None],
        gf[None],
        rows[:6],
        rows[6:],
        table.reshape(rel_bias.shape),
        total[16:20].reshape(D),
    )


def solution(mesh):
    return jax.shard_map(
        on_device,
        mesh=mesh,
        in_specs=(
            P("lev", "lat", "lon", None),
            P("lev", "lat", "lon", None),
            P("lat", "lon"),
            P(),
            P(),
            P(),
            P(),
            P(),
        ),
        out_specs=(
            P("lev", "lat", "lon", None),
            P("lev", "lat", "lon", None),
            P(("lon", "lat", "lev"), None),
            P(("lon", "lat", "lev"), None),
            P(),
            P(),
        ),
        check_vma=False,
    )
```

```python
import jax
import jax.numpy as jnp
import numpy as np
from jax import lax
from jax.experimental import pallas as pl
from jax.experimental.pallas import tpu as pltpu
from jax.sharding import PartitionSpec as P

MESH = pl.DeviceIdType.MESH
WROWS = 6
WCOLS = 12
WCELLS = WROWS * WCOLS
WPAD = 80
EPSILON = 1e-05
NEG_FILL = 100.0
D = 512
HEADS = 8
ROWS = 12
COLS = 48
HALO_ROWS = 5
HALO_COLS = 16
EXT_ROWS = ROWS + 2 * HALO_ROWS
EXT_COLS = COLS + 2 * HALO_COLS
KBLOCKS = ROWS // WROWS + 1
MBLOCKS = COLS // WCOLS + 1
STRIP = MBLOCKS * WPAD
LAT = 8
LON = 16
LEV = 2
MB = 1024 * 1024
NT = (((1,), (1,)), ((), ()))
TN = (((0,), (0,)), ((), ()))


def mm(a, b):
    return jnp.dot(a, b, preferred_element_type=jnp.float32)


def mm_nt(a, b):
    return lax.dot_general(a, b, NT, preferred_element_type=jnp.float32)


def mm_tn(a, b):
    return lax.dot_general(a, b, TN, preferred_element_type=jnp.float32)


UP, DOWN = 0, 1
LEFT, RIGHT = 0, 1
DIRECTIONS = [(dy, dx) for dy in (-1, 0, 1) for dx in (-1, 0, 1) if (dy, dx) != (0, 0)]
CENTRE = pl.ds(HALO_COLS, COLS)
FLAT = 256
OFFSETS = [(WROWS - 1) * (2 * WCOLS - 1) + WCOLS - 1 - (2 * WCOLS - 1) * (j // WCOLS) - j % WCOLS for j in range(WCELLS)]


def cell_tables():
    cell = np.arange(STRIP)
    m, t = cell // WPAD, cell % WPAD
    a, b = t // WCOLS, t % WCOLS
    real = t < WCELLS
    info = np.zeros((STRIP, 4), np.int32)
    info[:, 0] = np.where(real, a * EXT_COLS + WCOLS * m + b, -100000)
    info[:, 1] = np.where(real, a, -1000)
    info[:, 2] = np.where(real, WCOLS * m + b, -1000)
    info[:, 3] = real
    lanes = np.zeros((8, STRIP), np.int32)
    lanes[0] = np.where(real, a * COLS, -100000)
    lanes[1] = np.where(real, WCOLS * m + b, -100000)
    win = np.zeros((8, WPAD), np.int32)
    t = np.arange(WPAD)
    win[0] = np.where(t < WCELLS, t // WCOLS, -1000)
    win[1] = np.where(t < WCELLS, t % WCOLS, -1000)
    perm = np.zeros((64, 64), np.float32)
    for o in range(8):
        for r in range(6):
            perm[8 * o + r, 6 * o + r] = 1
        for r in range(2):
            perm[8 * o + 6 + r, 48 + 2 * o + r] = 1
    base = np.where(t < WCELLS, (2 * WCOLS - 1) * (t // WCOLS) + t % WCOLS, -1)
    obase = (np.arange(128)[:, None] == base[None, :]).astype(np.float32)
    return info, lanes, win, perm.astype(jnp.bfloat16), obase.astype(jnp.bfloat16)


def three_parts(x):
    hi = x.astype(jnp.bfloat16).astype(jnp.float32)
    rest = x - hi
    mid = rest.astype(jnp.bfloat16).astype(jnp.float32)
    return hi, mid, rest - mid


def normalized(x, gain):
    x = x.astype(jnp.float32)
    mean = jnp.mean(x, axis=-1, keepdims=True)
    cen = x - mean
    rstd = lax.rsqrt(jnp.mean(cen * cen, axis=-1, keepdims=True) + EPSILON)
    return mean, rstd, (cen * rstd * gain).astype(jnp.bfloat16)


def local_kernel(
    shift,
    f_ref,
    c_ref,
    m_ref,
    gain_ref,
    wqkv_ref,
    wproj_ref,
    rel_ref,
    info_ref,
    lanes_ref,
    win_ref,
    perm_ref,
    obase_ref,
    out_ref,
    gf_ref,
    part_ref,
    small_ref,
    tile_s,
    mx_s,
    vert_s,
    side_s,
    norm_s,
    cot_s,
    mean_s,
    rstd_s,
    rel_s,
    roll_s,
    bias_s,
    g_s,
    z_s,
    pick_s,
    put_s,
    key_s,
    qkv_s,
    gm_s,
    mix_s,
    gc_s,
    mixo_s,
    gco_s,
    send,
    recv,
):
    bf = jnp.bfloat16
    f32 = jnp.float32
    lon = lax.axis_index("lon")
    lat = lax.axis_index("lat")
    lev = lax.axis_index("lev")
    lat_shift = 1 + jnp.mod(shift[0], WROWS - 1)
    lon_shift = 1 + jnp.mod(shift[1], WCOLS - 1)
    lat_base = lat * ROWS
    has_above = lat > 0
    has_below = lat < LAT - 1
    true = lat >= 0

    def neighbour(dy, dx):
        return (lax.rem(lon + dx + LON, LON), lat + dy, lev)

    def exists(dy):
        return {-1: has_above, 0: true, 1: has_below}[dy]

    def remote(src, dst, n, to):
        return pltpu.make_async_remote_copy(
            src_ref=src, dst_ref=dst, send_sem=send.at[n], recv_sem=recv.at[n], device_id=to, device_id_type=MESH
        )

    barrier = pltpu.get_barrier_semaphore()
    for dy, dx in DIRECTIONS:

        @pl.when(exists(dy))
        def _(dy=dy, dx=dx):
            pl.semaphore_signal(barrier, inc=1, device_id=neighbour(dy, dx), device_id_type=MESH)

    tile_s[...] = jnp.zeros_like(tile_s)
    tile_s[:ROWS, :COLS] = m_ref[...].astype(f32)
    mx_s[1, 1] = tile_s[...]
    for absent, rows in ((lat == 0, UP), (lat == LAT - 1, DOWN)):

        @pl.when(absent)
        def _(rows=rows):
            vert_s[:, rows] = jnp.zeros_like(vert_s[:, rows])
            for block in range(3):
                mx_s[block, 2 * rows] = jnp.zeros((16, 128), f32)

    @pl.when(has_above & has_below)
    def _():
        pl.semaphore_wait(barrier, 8)

    @pl.when(~(has_above & has_below))
    def _():
        pl.semaphore_wait(barrier, 5)

    masks = []
    for n, (dy, dx) in enumerate(DIRECTIONS):
        copy = remote(tile_s, mx_s.at[1 - dx, 1 - dy], n, neighbour(dy, dx))
        masks.append((copy, exists(dy), exists(-dy)))
    vertical = [[], []]
    sides = [[], []]
    corners = [[], []]
    for i, src in enumerate((f_ref, c_ref)):
        for way, dy, rows in (
            (DOWN, -1, pl.ds(0, HALO_ROWS)),
            (UP, 1, pl.ds(ROWS - HALO_ROWS, HALO_ROWS)),
        ):
            copy = remote(src.at[rows], vert_s.at[i, way, :, CENTRE], 8 + 2 * way + i, neighbour(dy, 0))
            vertical[i].append((copy, exists(dy), exists(-dy)))
        for s, dx, cols in ((LEFT, 1, pl.ds(COLS - HALO_COLS, HALO_COLS)), (RIGHT, -1, pl.ds(0, HALO_COLS))):
            sides[i].append(remote(src.at[:, cols], side_s.at[i, s], 12 + 2 * s + i, neighbour(0, dx)))
        for way, there in ((UP, has_above), (DOWN, has_below)):
            for s, dx, cols, dst in (
                (LEFT, 1, pl.ds(COLS, HALO_COLS), pl.ds(0, HALO_COLS)),
                (RIGHT, -1, pl.ds(HALO_COLS, HALO_COLS), pl.ds(HALO_COLS + COLS, HALO_COLS)),
            ):
                n = 16 + 4 * way + 2 * s + i
                copy = remote(vert_s.at[i, way, :, cols], vert_s.at[i, way, :, dst], n, neighbour(0, dx))
                corners[i].append((copy, there))
    for copy, sends, _ in masks:
        pl.when(sends)(copy.start)
    for i in range(2):
        for copy, sends, _ in vertical[i]:
            pl.when(sends)(copy.start)
        for copy in sides[i]:
            copy.start()

    def pass_corners(i):
        for copy, _, receives in vertical[i]:
            pl.when(receives)(copy.wait_recv)
        for copy, there in corners[i]:
            pl.when(there)(copy.start)

    gain = gain_ref[...]
    half = lax.broadcasted_iota(jnp.int32, (1, 128), 1) < 64
    lane4 = lax.broadcasted_iota(jnp.int32, (1, 256), 1)
    head_masks = [
        jnp.where((lane4 >= 64 * h) & (lane4 < 64 * h + 64), 1.0, 0.0).astype(bf) for h in range(4)
    ]
    g_s[...] = jnp.zeros_like(g_s)

    mean, rstd, norm = normalized(f_ref[...].reshape(ROWS * COLS, D), gain)
    mean_s[...] = mean
    rstd_s[...] = rstd
    own_rows = slice(HALO_ROWS, HALO_ROWS + ROWS)
    own_cols = slice(HALO_COLS, HALO_COLS + COLS)
    norm_s[own_rows, own_cols] = norm.reshape(ROWS, COLS, D)
    cot_s[own_rows, own_cols] = c_ref[...]

    rel_s[...] = jnp.zeros_like(rel_s)
    flat = jnp.zeros((HEADS, FLAT), f32)
    for u in range(2 * WROWS - 1):
        rel_s[u, :, : 2 * WCOLS - 1] = rel_ref[u]
        flat = flat + pltpu.roll(rel_s[u], (2 * WCOLS - 1) * u, 1)
    rel3 = jnp.concatenate(three_parts(flat), axis=0)
    for j in range(WCELLS):
        roll_s[j] = pltpu.roll(rel3, (FLAT - OFFSETS[j]) % FLAT, 1)[:, :128]
    pairs = mm(roll_s[...].reshape(WCELLS * 24, 128).astype(bf), obase_ref[...])
    pairs = pairs.reshape(WCELLS, 24, WPAD)
    pairs = (pairs[:, 16:24] + pairs[:, 8:16]) + pairs[:, :8]
    bias_s[...] = jnp.zeros_like(bias_s)
    for j in range(WCELLS):
        bias_s[:, j, :] = pairs[j]

    acol = info_ref[:, 1:2]
    valid = []
    for k in range(KBLOCKS):
        grow = acol + (lat_shift - WROWS + WROWS * k + lat_base)
        valid.append((grow >= 0) & (grow < LAT * ROWS))
        target = jnp.where(valid[k], info_ref[:, 0:1] + (lon_shift + 4), -1)
        lane = lax.broadcasted_iota(jnp.int32, (STRIP, WROWS * EXT_COLS), 1)
        pick_s[k] = jnp.where(lane == target, 1.0, 0.0).astype(bf)
    xl = lanes_ref[1:2, :] + (lon_shift - WCOLS)
    place = jnp.where((xl >= 0) & (xl < COLS), lanes_ref[0:1, :] + xl, -1)
    sub = lax.broadcasted_iota(jnp.int32, (WROWS * COLS, STRIP), 0)
    put_s[...] = jnp.where(sub == place, 1.0, 0.0).astype(bf)

    for copy, sends, receives in masks:
        pl.when(sends)(copy.wait_send)
        pl.when(receives)(copy.wait_recv)
    xcol = info_ref[:, 2:3] + (lon_shift + 4)
    lane = lax.broadcasted_iota(jnp.int32, (STRIP, 128), 1)
    by_row = 0.0
    for block, offset in enumerate((32, -16, -64)):
        mpick = jnp.where(lane == xcol + offset, 1.0, 0.0).astype(bf)
        by_row = by_row + mm_nt(mpick, mx_s[block].reshape(48, 128).astype(bf))
    lane = lax.broadcasted_iota(jnp.int32, (STRIP, 48), 1)
    for k in range(KBLOCKS):
        erow = acol + (lat_shift - 1 + WROWS * k)
        flat = jnp.where(erow < 5, erow + 7, jnp.where(erow < 17, erow + 11, erow + 15))
        keep = jnp.sum(jnp.where((lane == flat) & valid[k], by_row, 0.0), axis=-1, keepdims=True)
        key_s[k] = jnp.where(info_ref[:, 3:4] > 0, NEG_FILL * (keep - 1.0), -1e30)

    def rows_of(k):
        return pl.ds(lat_shift - 1 + WROWS * k, WROWS)

    def strip(k, between=None):
        norm = norm_s[rows_of(k)].reshape(WROWS * EXT_COLS, D)
        cot = cot_s[rows_of(k)].reshape(WROWS * EXT_COLS, D)
        nw = mm(pick_s[k], norm).astype(bf)
        cw = mm(pick_s[k], cot).astype(bf)
        qkv = mm_nt(nw, wqkv_ref[...]).astype(bf)
        qkv_s[:, :D] = qkv[:, :D] * jnp.asarray(0.125, bf)
        qkv_s[:, D:] = qkv[:, D:]
        gm_s[...] = mm(cw, wproj_ref[...]).astype(bf)
        win_row = win_ref[0:1, :] + (lat_shift - WROWS + WROWS * k)
        row_own = (win_row >= 0) & (win_row < ROWS)
        for m in range(MBLOCKS):
            if between is not None and m in between:
                between[m]()
            sl = slice(m * WPAD, m * WPAD + WPAD)
            key = key_s[k, sl, :]
            win_col = win_ref[1:2, :] + (lon_shift - WCOLS + WCOLS * m)
            own = jnp.where(row_own & (win_col >= 0) & (win_col < COLS), 1.0, 0.0)
            for q in range(2):
                lo = 256 * q
                qq = qkv_s[sl, lo : lo + 256]
                kq = qkv_s[sl, D + lo : D + lo + 256]
                vq = qkv_s[sl, 2 * D + lo : 2 * D + lo + 256]
                mq = gm_s[sl, lo : lo + 256]
                kst = jnp.concatenate([kq * h for h in head_masks], axis=0)
                vst = jnp.concatenate([vq * h for h in head_masks], axis=0)
                st = mm_nt(kst, qq).reshape(4, WPAD, WPAD)
                st = (st + bias_s[4 * q : 4 * q + 4]) + key[None]
                top = jnp.max(st, axis=1, keepdims=True)
                ex = jnp.exp(st - top)
                pr = ex * (1.0 / jnp.sum(ex, axis=1, keepdims=True))
                prh = pr.astype(bf).reshape(4 * WPAD, WPAD)
                gp = mm_nt(vst, mq).reshape(4, WPAD, WPAD)
                pg = pr * gp
                ds = pr * (gp - jnp.sum(pg, axis=1, keepdims=True))
                g_s[4 * q : 4 * q + 4] += ds * own[None]
                dsh = ds.astype(bf).reshape(4 * WPAD, WPAD)
                mix_s[sl, lo : lo + 256] = mm_tn(prh, vst).astype(bf)
                gc_s[sl, lo : lo + 256] = (mm_tn(dsh, kst) * 0.125).astype(bf)
                gk = mm(dsh, qq).reshape(4, WPAD, 256)
                gv = mm(prh, mq).reshape(4, WPAD, 256)
                for s, base in ((gk, D), (gv, 2 * D)):
                    for c in range(2):
                        lanes = slice(128 * c, 128 * c + 128)
                        both = jnp.where(half, s[2 * c, :, lanes], s[2 * c + 1, :, lanes])
                        gc_s[sl, base + lo + 128 * c : base + lo + 128 * c + 128] = both.astype(bf)
        rows = slice(WROWS * k, WROWS * k + WROWS)
        mixo_s[rows] = mm(put_s[...], mix_s[...]).astype(bf).reshape(WROWS, COLS, D)
        gco_s[rows] = mm(put_s[...], gc_s[...]).astype(bf).reshape(WROWS, COLS, 3 * D)

    side_cols = ((LEFT, slice(0, HALO_COLS)), (RIGHT, slice(HALO_COLS + COLS, EXT_COLS)))
    end_rows = ((UP, slice(0, HALO_ROWS)), (DOWN, slice(HALO_ROWS + ROWS, EXT_ROWS)))
    for copy in sides[0] + sides[1]:
        copy.wait()
    for s, cols in side_cols:
        norm = normalized(side_s[0, s].reshape(ROWS * HALO_COLS, D), gain)[2]
        norm_s[own_rows, cols] = norm.reshape(ROWS, HALO_COLS, D)
        cot_s[own_rows, cols] = side_s[1, s]
    strip(1, {2: lambda: pass_corners(0), 4: lambda: pass_corners(1)})
    for copy, there in corners[0] + corners[1]:
        pl.when(there)(copy.wait)
    for way, rows in end_rows:
        norm = normalized(vert_s[0, way].reshape(HALO_ROWS * EXT_COLS, D), gain)[2]
        norm_s[rows] = norm.reshape(HALO_ROWS, EXT_COLS, D)
        cot_s[rows] = vert_s[1, way]
    strip(0)
    strip(2)
    for i in range(2):
        for copy, sends, _ in vertical[i]:
            pl.when(sends)(copy.wait_send)

    cells = ROWS * COLS
    first = pl.ds(WROWS - lat_shift, ROWS)
    x = f_ref[...].reshape(cells, D).astype(f32)
    cot = c_ref[...].reshape(cells, D)
    norm = norm_s[own_rows, own_cols].reshape(cells, D)
    mean = mean_s[...]
    rstd = rstd_s[...]
    mixo = mixo_s[first].reshape(cells, D)
    gco = gco_s[first].reshape(cells, 3 * D)
    out_ref[...] = (x + mm_nt(mixo, wproj_ref[...])).astype(bf).reshape(ROWS, COLS, D)
    gn = mm(gco, wqkv_ref[...])
    xhat = (x - mean) * rstd
    gg = jnp.sum(gn * xhat, axis=0, keepdims=True)
    gs = gn * gain
    gin = rstd * (
        gs
        - jnp.mean(gs, axis=-1, keepdims=True)
        - xhat * jnp.mean(gs * xhat, axis=-1, keepdims=True)
    )
    gf_ref[...] = (cot.astype(f32) + gin).astype(bf).reshape(ROWS, COLS, D)
    gq = mm_tn(gco, norm).astype(bf)
    gp = mm_tn(cot, mixo).astype(bf)
    for o in range(32):
        rows = jnp.concatenate([gq[48 * o : 48 * o + 48], gp[16 * o : 16 * o + 16]], axis=0)
        part_ref[64 * o : 64 * o + 64] = mm(perm_ref[...], rows).astype(bf)

    small_ref[...] = jnp.zeros_like(small_ref)
    parts = three_parts(g_s[...].reshape(HEADS * WPAD, WPAD))
    z = mm_nt(parts[2].astype(bf), obase_ref[...]) + mm_nt(parts[1].astype(bf), obase_ref[...])
    z = z + mm_nt(parts[0].astype(bf), obase_ref[...])
    z_s[...] = z.reshape(HEADS, WPAD, 128)
    zero = jnp.zeros((HEADS, 128), f32)
    table = jnp.zeros((HEADS, FLAT), f32)
    for j in range(WCELLS):
        wide = jnp.concatenate([z_s[:, j, :], zero], axis=1)
        table = table + pltpu.roll(wide, OFFSETS[j], 1)
    small_ref[0:4, :] = jnp.concatenate([table[0:4], table[4:8]], axis=1)
    small_ref[4:5, :] = gg


def local(shift, fields, cotangent, mask, gain, w_qkv, w_proj, rel):
    info, lanes, win, perm, obase = cell_tables()
    vmem = pl.BlockSpec(memory_space=pltpu.VMEM)
    smem = pl.BlockSpec(memory_space=pltpu.SMEM)
    tile = jax.ShapeDtypeStruct((ROWS, COLS, D), jnp.bfloat16)
    bf = jnp.bfloat16
    f32 = jnp.float32
    vm = pltpu.VMEM
    dma = pltpu.SemaphoreType.DMA
    strip_rows = KBLOCKS * WROWS
    return pl.pallas_call(
        local_kernel,
        out_shape=(
            tile,
            tile,
            jax.ShapeDtypeStruct((2048, D), bf),
            jax.ShapeDtypeStruct((8, D), f32),
        ),
        in_specs=[smem] + [vmem] * 12,
        out_specs=(vmem,) * 4,
        scratch_shapes=[
            vm((16, 128), f32),
            vm((3, 3, 16, 128), f32),
            vm((2, 2, HALO_ROWS, EXT_COLS, D), bf),
            vm((2, 2, ROWS, HALO_COLS, D), bf),
            vm((EXT_ROWS, EXT_COLS, D), bf),
            vm((EXT_ROWS, EXT_COLS, D), bf),
            vm((ROWS * COLS, 1), f32),
            vm((ROWS * COLS, 1), f32),
            vm((2 * WROWS - 1, HEADS, FLAT), f32),
            vm((WCELLS, 24, 128), f32),
            vm((HEADS, WPAD, WPAD), f32),
            vm((HEADS, WPAD, WPAD), f32),
            vm((HEADS, WPAD, 128), f32),
            vm((KBLOCKS, STRIP, WROWS * EXT_COLS), bf),
            vm((WROWS * COLS, STRIP), bf),
            vm((KBLOCKS, STRIP, 1), f32),
            vm((STRIP, 3 * D), bf),
            vm((STRIP, D), bf),
            vm((STRIP, D), bf),
            vm((STRIP, 3 * D), bf),
            vm((strip_rows, COLS, D), bf),
            vm((strip_rows, COLS, 3 * D), bf),
            dma((24,)),
            dma((24,)),
        ],
        compiler_params=pltpu.CompilerParams(
            collective_id=0, has_side_effects=True, vmem_limit_bytes=56 * MB
        ),
        name="window_attention",
    )(
        shift, fields, cotangent, mask, gain, w_qkv, w_proj, rel,
        jnp.asarray(info), jnp.asarray(lanes), jnp.asarray(win), jnp.asarray(perm), jnp.asarray(obase),
    )


PLANE = 16
ZED = 8


def as_pair(x):
    hi = x.astype(jnp.bfloat16).astype(jnp.float32)
    return jnp.concatenate([hi, x - hi], axis=0).astype(jnp.bfloat16)


def reduce_kernel(
    part_ref, small_ref, rows_ref, total_ref,
    own_a, got_a, small_a, buf_b, got_b, buf_c, got_c,
    load_a, send_a, recv_a, send_b, recv_b, send_c, recv_c,
):
    bf = jnp.bfloat16
    f32 = jnp.float32
    lon = lax.axis_index("lon")
    lat = lax.axis_index("lat")
    lev = lax.axis_index("lev")
    zed = lon // 2
    core = lax.rem(lon, 2)
    plane = lat * 2 + lev
    sibling = (zed * 2 + (1 - core), lat, lev)

    def in_plane(p):
        return (lon, p // 2, lax.rem(p, 2))

    def along_z(z):
        return (z * 2 + core, lat, lev)

    barrier = pltpu.get_barrier_semaphore()
    pl.semaphore_signal(barrier, inc=1, device_id=sibling, device_id_type=MESH)
    for d in range(1, PLANE):
        p = lax.rem(plane + d, PLANE)
        pl.semaphore_signal(barrier, inc=1, device_id=in_plane(p), device_id_type=MESH)
    for d in range(1, ZED):
        z = lax.rem(zed + d, ZED)
        pl.semaphore_signal(barrier, inc=1, device_id=along_z(z), device_id_type=MESH)

    def remote(src, dst, send, recv, to):
        return pltpu.make_async_remote_copy(
            src_ref=src, dst_ref=dst, send_sem=send, recv_sem=recv, device_id=to, device_id_type=MESH
        )

    chunks = []
    for c in range(4):
        rows = pl.ds(pl.multiple_of(32 * lax.rem(plane // 4 + c, 4), 32), 32)
        there = remote(part_ref.at[:, 1 - core, rows], got_a.at[:, rows], send_a.at[c], recv_a.at[c], sibling)
        here = pltpu.make_async_copy(part_ref.at[:, core, rows], own_a.at[:, rows], load_a.at[c])
        here.start()
        chunks.append((there, here, rows))
    pl.semaphore_wait(barrier, 1 + PLANE - 1 + ZED - 1)
    copy_s = remote(small_ref, small_a, send_a.at[4], recv_a.at[4], sibling)
    copy_s.start()
    for there, _, _ in chunks:
        there.start()
    copy_s.wait()
    pair = as_pair(small_ref[...] + small_a[...])
    for p in range(PLANE):
        buf_b[p, 64:80] = pair

    def to_plane(p):
        return remote(buf_b.at[p], got_b.at[plane], send_b.at[p], recv_b.at[plane], in_plane(p))

    for c, (there, here, rows) in enumerate(chunks):
        here.wait()
        there.wait()
        base = 4 * lax.rem(plane // 4 + c, 4)
        for z in range(0, ZED, 2):
            lo = own_a[z, rows].astype(f32) + got_a[z, rows].astype(f32)
            hi = own_a[z + 1, rows].astype(f32) + got_a[z + 1, rows].astype(f32)
            both = jnp.concatenate([lo.reshape(4, 8, D), hi.reshape(4, 8, D)], axis=1)
            buf_b[pl.ds(base, 4), 8 * z : 8 * z + 16] = both.astype(bf)
        for e in range(4):
            p = base + lax.rem(plane + e, 4)

            @pl.when(p != plane)
            def _(p=p):
                to_plane(p).start()

    got_b[plane, 64:80] = pair
    acc = buf_b[plane, 0:64].astype(f32)
    for d in range(1, PLANE):
        p = lax.rem(plane + d, PLANE)
        remote(buf_b.at[p], got_b.at[p], send_b.at[p], recv_b.at[p], in_plane(p)).wait()
        acc = acc + got_b[p, 0:64].astype(f32)
    total = jnp.zeros((16, D), f32)
    for p in range(PLANE):
        total = total + got_b[p, 64:80].astype(f32)
    pair = as_pair(total[:8] + total[8:])

    for z in range(ZED):
        piece = acc[8 * z : 8 * z + 8]
        buf_c[z, 0:16] = jnp.concatenate([piece[:, :256], piece[:, 256:]], axis=0).astype(bf)
        buf_c[z, 16:32] = pair[:, :256]
        buf_c[z, 32:48] = pair[:, 256:]

    def along(z):
        return remote(buf_c.at[z], got_c.at[zed], send_c.at[z], recv_c.at[zed], along_z(z))

    for d in range(1, ZED):
        along(lax.rem(zed + d, ZED)).start()
    got_c[zed] = buf_c[zed]
    for d in range(1, ZED):
        z = lax.rem(zed + d, ZED)
        remote(buf_c.at[z], got_c.at[z], send_c.at[z], recv_c.at[z], along_z(z)).wait()
    total = got_c[0].astype(f32)
    for z in range(1, ZED):
        total = total + got_c[z].astype(f32)
    rows_ref[:, :256] = total[0:8]
    rows_ref[:, 256:] = total[8:16]
    total_ref[:, :256] = total[16:24] + total[24:32]
    total_ref[:, 256:] = total[32:40] + total[40:48]


def reduce_all(part, small):
    vmem = pl.BlockSpec(memory_space=pltpu.VMEM)
    f32 = jnp.float32
    bf = jnp.bfloat16
    vm = pltpu.VMEM
    dma = pltpu.SemaphoreType.DMA
    return pl.pallas_call(
        reduce_kernel,
        out_shape=(jax.ShapeDtypeStruct((8, D), f32), jax.ShapeDtypeStruct((8, D), f32)),
        in_specs=[pl.BlockSpec(memory_space=pl.ANY), vmem],
        out_specs=(vmem,) * 2,
        scratch_shapes=[
            vm((ZED, 128, D), bf),
            vm((ZED, 128, D), bf),
            vm((8, D), f32),
            vm((PLANE, 80, D), bf),
            vm((PLANE, 80, D), bf),
            vm((ZED, 48, 256), bf),
            vm((ZED, 48, 256), bf),
            dma((4,)),
            dma((5,)),
            dma((5,)),
            dma((PLANE,)),
            dma((PLANE,)),
            dma((ZED,)),
            dma((ZED,)),
        ],
        compiler_params=pltpu.CompilerParams(
            collective_id=1, has_side_effects=True, vmem_limit_bytes=60 * MB
        ),
        name="reduce_gradients",
    )(part.reshape(ZED, 2, 128, D), small)


def on_device(fields, cotangent, land_mask, shift_offsets, norm_gain, w_qkv, w_proj, rel_bias):
    entries = rel_bias.shape[1] * rel_bias.shape[2]
    rel = rel_bias.transpose(1, 0, 2)
    out, gf, part, small = local(
        shift_offsets, fields[0], cotangent[0], land_mask, norm_gain.reshape(1, D), w_qkv, w_proj, rel
    )
    rows, total = reduce_all(part, small)
    table = jnp.concatenate([total[0:4, :FLAT], total[0:4, FLAT:]], axis=0)[:, :entries]
    return (
        out[None],
        gf[None],
        rows[:6],
        rows[6:],
        table.reshape(rel_bias.shape),
        total[4],
    )


def solution(mesh):
    return jax.shard_map(
        on_device,
        mesh=mesh,
        in_specs=(
            P("lev", "lat", "lon", None),
            P("lev", "lat", "lon", None),
            P("lat", "lon"),
            P(),
            P(),
            P(),
            P(),
            P(),
        ),
        out_specs=(
            P("lev", "lat", "lon", None),
            P("lev", "lat", "lon", None),
            P(("lon", "lat", "lev"), None),
            P(("lon", "lat", "lev"), None),
            P(),
            P(),
        ),
        check_vma=False,
    )
```

```python
import jax
import jax.numpy as jnp
import numpy as np
from jax import lax
from jax.experimental import pallas as pl
from jax.experimental.pallas import tpu as pltpu
from jax.sharding import PartitionSpec as P

MESH = pl.DeviceIdType.MESH
WROWS = 6
WCOLS = 12
WCELLS = WROWS * WCOLS
WPAD = 80
EPSILON = 1e-05
NEG_FILL = 100.0
D = 512
HEADS = 8
ROWS = 12
COLS = 48
HALO_ROWS = 5
HALO_COLS = 16
EXT_ROWS = ROWS + 2 * HALO_ROWS
EXT_COLS = COLS + 2 * HALO_COLS
KBLOCKS = ROWS // WROWS + 1
MBLOCKS = COLS // WCOLS + 1
STRIP = MBLOCKS * WPAD
LAT = 8
LON = 16
LEV = 2
MAIN = 384
MB = 1024 * 1024
NT = (((1,), (1,)), ((), ()))
TN = (((0,), (0,)), ((), ()))


def mm(a, b):
    return jnp.dot(a, b, preferred_element_type=jnp.float32)


def mm_nt(a, b):
    return lax.dot_general(a, b, NT, preferred_element_type=jnp.float32)


def mm_tn(a, b):
    return lax.dot_general(a, b, TN, preferred_element_type=jnp.float32)


UP, DOWN = 0, 1
LEFT, RIGHT = 0, 1
DIRECTIONS = [(dy, dx) for dy in (-1, 0, 1) for dx in (-1, 0, 1) if (dy, dx) != (0, 0)]
CENTRE = pl.ds(HALO_COLS, COLS)
FLAT = 256
OFFSETS = [(WROWS - 1) * (2 * WCOLS - 1) + WCOLS - 1 - (2 * WCOLS - 1) * (j // WCOLS) - j % WCOLS for j in range(WCELLS)]


def cell_tables():
    cell = np.arange(STRIP)
    m, t = cell // WPAD, cell % WPAD
    a, b = t // WCOLS, t % WCOLS
    real = t < WCELLS
    info = np.zeros((STRIP, 4), np.int32)
    info[:, 0] = np.where(real, a * EXT_COLS + WCOLS * m + b, -100000)
    info[:, 1] = np.where(real, a, -1000)
    info[:, 2] = np.where(real, WCOLS * m + b, -1000)
    info[:, 3] = real
    lanes = np.zeros((8, STRIP), np.int32)
    lanes[0] = np.where(real, a * COLS, -100000)
    lanes[1] = np.where(real, WCOLS * m + b, -100000)
    win = np.zeros((8, WPAD), np.int32)
    t = np.arange(WPAD)
    win[0] = np.where(t < WCELLS, t // WCOLS, -1000)
    win[1] = np.where(t < WCELLS, t % WCOLS, -1000)
    perm = np.zeros((64, 64), np.float32)
    for o in range(8):
        for r in range(6):
            perm[8 * o + r, 6 * o + r] = 1
        for r in range(2):
            perm[8 * o + 6 + r, 48 + 2 * o + r] = 1
    base = np.where(t < WCELLS, (2 * WCOLS - 1) * (t // WCOLS) + t % WCOLS, -1)
    obase = (np.arange(128)[:, None] == base[None, :]).astype(np.float32)
    return info, lanes, win, perm.astype(jnp.bfloat16), obase.astype(jnp.bfloat16)


def three_parts(x):
    hi = x.astype(jnp.bfloat16).astype(jnp.float32)
    rest = x - hi
    mid = rest.astype(jnp.bfloat16).astype(jnp.float32)
    return hi, mid, rest - mid


def normalized(x, gain):
    x = x.astype(jnp.float32)
    mean = jnp.mean(x, axis=-1, keepdims=True)
    cen = x - mean
    rstd = lax.rsqrt(jnp.mean(cen * cen, axis=-1, keepdims=True) + EPSILON)
    return mean, rstd, (cen * rstd * gain).astype(jnp.bfloat16)


def local_kernel(
    shift,
    f_ref,
    c_ref,
    m_ref,
    gain_ref,
    wqkv_ref,
    wproj_ref,
    rel_ref,
    info_ref,
    lanes_ref,
    win_ref,
    perm_ref,
    obase_ref,
    out_ref,
    gf_ref,
    part_ref,
    small_ref,
    tile_s,
    mx_s,
    vert_s,
    side_s,
    norm_s,
    cot_s,
    mean_s,
    rstd_s,
    rel_s,
    roll_s,
    bias_s,
    g_s,
    z_s,
    pick_s,
    put_s,
    key_s,
    qkv_s,
    gm_s,
    mix_s,
    gc_s,
    mixo_s,
    gco_s,
    send,
    recv,
):
    bf = jnp.bfloat16
    f32 = jnp.float32
    lon = lax.axis_index("lon")
    lat = lax.axis_index("lat")
    lev = lax.axis_index("lev")
    lat_shift = 1 + jnp.mod(shift[0], WROWS - 1)
    lon_shift = 1 + jnp.mod(shift[1], WCOLS - 1)
    lat_base = lat * ROWS
    has_above = lat > 0
    has_below = lat < LAT - 1
    true = lat >= 0

    def neighbour(dy, dx):
        return (lax.rem(lon + dx + LON, LON), lat + dy, lev)

    def exists(dy):
        return {-1: has_above, 0: true, 1: has_below}[dy]

    def remote(src, dst, n, to):
        return pltpu.make_async_remote_copy(
            src_ref=src, dst_ref=dst, send_sem=send.at[n], recv_sem=recv.at[n], device_id=to, device_id_type=MESH
        )

    barrier = pltpu.get_barrier_semaphore()
    for dy, dx in DIRECTIONS:

        @pl.when(exists(dy))
        def _(dy=dy, dx=dx):
            pl.semaphore_signal(barrier, inc=1, device_id=neighbour(dy, dx), device_id_type=MESH)

    tile_s[...] = jnp.zeros_like(tile_s)
    tile_s[:ROWS, :COLS] = m_ref[...].astype(f32)
    mx_s[1, 1] = tile_s[...]
    for absent, rows in ((lat == 0, UP), (lat == LAT - 1, DOWN)):

        @pl.when(absent)
        def _(rows=rows):
            vert_s[:, rows] = jnp.zeros_like(vert_s[:, rows])
            for block in range(3):
                mx_s[block, 2 * rows] = jnp.zeros((16, 128), f32)

    @pl.when(has_above & has_below)
    def _():
        pl.semaphore_wait(barrier, 8)

    @pl.when(~(has_above & has_below))
    def _():
        pl.semaphore_wait(barrier, 5)

    masks = []
    for n, (dy, dx) in enumerate(DIRECTIONS):
        copy = remote(tile_s, mx_s.at[1 - dx, 1 - dy], n, neighbour(dy, dx))
        masks.append((copy, exists(dy), exists(-dy)))
    vertical = [[], []]
    sides = [[], []]
    corners = [[], []]
    for i, src in enumerate((f_ref, c_ref)):
        for way, dy, rows in (
            (DOWN, -1, pl.ds(0, HALO_ROWS)),
            (UP, 1, pl.ds(ROWS - HALO_ROWS, HALO_ROWS)),
        ):
            copy = remote(src.at[rows], vert_s.at[i, way, :, CENTRE], 8 + 2 * way + i, neighbour(dy, 0))
            vertical[i].append((copy, exists(dy), exists(-dy)))
        for s, dx, cols in ((LEFT, 1, pl.ds(COLS - HALO_COLS, HALO_COLS)), (RIGHT, -1, pl.ds(0, HALO_COLS))):
            sides[i].append(remote(src.at[:, cols], side_s.at[i, s], 12 + 2 * s + i, neighbour(0, dx)))
        for way, there in ((UP, has_above), (DOWN, has_below)):
            for s, dx, cols, dst in (
                (LEFT, 1, pl.ds(COLS, HALO_COLS), pl.ds(0, HALO_COLS)),
                (RIGHT, -1, pl.ds(HALO_COLS, HALO_COLS), pl.ds(HALO_COLS + COLS, HALO_COLS)),
            ):
                n = 16 + 4 * way + 2 * s + i
                copy = remote(vert_s.at[i, way, :, cols], vert_s.at[i, way, :, dst], n, neighbour(0, dx))
                corners[i].append((copy, there))
    for copy, sends, _ in masks:
        pl.when(sends)(copy.start)
    for i in range(2):
        for copy, sends, _ in vertical[i]:
            pl.when(sends)(copy.start)
        for copy in sides[i]:
            copy.start()

    def pass_corners(i):
        for copy, _, receives in vertical[i]:
            pl.when(receives)(copy.wait_recv)
        for copy, there in corners[i]:
            pl.when(there)(copy.start)

    gain = gain_ref[...]
    half = lax.broadcasted_iota(jnp.int32, (1, 128), 1) < 64
    lane4 = lax.broadcasted_iota(jnp.int32, (1, 256), 1)
    head_masks = [
        jnp.where((lane4 >= 64 * h) & (lane4 < 64 * h + 64), 1.0, 0.0).astype(bf) for h in range(4)
    ]
    g_s[...] = jnp.zeros_like(g_s)

    mean, rstd, norm = normalized(f_ref[...].reshape(ROWS * COLS, D), gain)
    mean_s[...] = mean
    rstd_s[...] = rstd
    own_rows = slice(HALO_ROWS, HALO_ROWS + ROWS)
    own_cols = slice(HALO_COLS, HALO_COLS + COLS)
    norm_s[own_rows, own_cols] = norm.reshape(ROWS, COLS, D)
    cot_s[own_rows, own_cols] = c_ref[...]

    rel_s[...] = jnp.zeros_like(rel_s)
    flat = jnp.zeros((HEADS, FLAT), f32)
    for u in range(2 * WROWS - 1):
        rel_s[u, :, : 2 * WCOLS - 1] = rel_ref[u]
        flat = flat + pltpu.roll(rel_s[u], (2 * WCOLS - 1) * u, 1)
    rel3 = jnp.concatenate(three_parts(flat), axis=0)
    for j in range(WCELLS):
        roll_s[j] = pltpu.roll(rel3, (FLAT - OFFSETS[j]) % FLAT, 1)[:, :128]
    pairs = mm(roll_s[...].reshape(WCELLS * 24, 128).astype(bf), obase_ref[...])
    pairs = pairs.reshape(WCELLS, 24, WPAD)
    pairs = (pairs[:, 16:24] + pairs[:, 8:16]) + pairs[:, :8]
    bias_s[...] = jnp.zeros_like(bias_s)
    for j in range(WCELLS):
        bias_s[:, j, :] = pairs[j]

    acol = info_ref[:, 1:2]
    valid = []
    for k in range(KBLOCKS):
        grow = acol + (lat_shift - WROWS + WROWS * k + lat_base)
        valid.append((grow >= 0) & (grow < LAT * ROWS))
        target = jnp.where(valid[k], info_ref[:, 0:1] + (lon_shift + 4), -1)
        lane = lax.broadcasted_iota(jnp.int32, (STRIP, WROWS * EXT_COLS), 1)
        pick_s[k] = jnp.where(lane == target, 1.0, 0.0).astype(bf)
    xl = lanes_ref[1:2, :] + (lon_shift - WCOLS)
    place = jnp.where((xl >= 0) & (xl < COLS), lanes_ref[0:1, :] + xl, -1)
    sub = lax.broadcasted_iota(jnp.int32, (WROWS * COLS, STRIP), 0)
    put_s[...] = jnp.where(sub == place, 1.0, 0.0).astype(bf)

    for copy, sends, receives in masks:
        pl.when(sends)(copy.wait_send)
        pl.when(receives)(copy.wait_recv)
    xcol = info_ref[:, 2:3] + (lon_shift + 4)
    lane = lax.broadcasted_iota(jnp.int32, (STRIP, 128), 1)
    by_row = 0.0
    for block, offset in enumerate((32, -16, -64)):
        mpick = jnp.where(lane == xcol + offset, 1.0, 0.0).astype(bf)
        by_row = by_row + mm_nt(mpick, mx_s[block].reshape(48, 128).astype(bf))
    lane = lax.broadcasted_iota(jnp.int32, (STRIP, 48), 1)
    for k in range(KBLOCKS):
        erow = acol + (lat_shift - 1 + WROWS * k)
        flat = jnp.where(erow < 5, erow + 7, jnp.where(erow < 17, erow + 11, erow + 15))
        keep = jnp.sum(jnp.where((lane == flat) & valid[k], by_row, 0.0), axis=-1, keepdims=True)
        key_s[k] = jnp.where(info_ref[:, 3:4] > 0, NEG_FILL * (keep - 1.0), -1e30)

    def rows_of(k):
        return pl.ds(lat_shift - 1 + WROWS * k, WROWS)

    def strip(k, between=None):
        norm = norm_s[rows_of(k)].reshape(WROWS * EXT_COLS, D)
        cot = cot_s[rows_of(k)].reshape(WROWS * EXT_COLS, D)
        nw = mm(pick_s[k], norm).astype(bf)
        cw = mm(pick_s[k], cot).astype(bf)
        qkv = mm_nt(nw, wqkv_ref[...]).astype(bf)
        qkv_s[:, :D] = qkv[:, :D] * jnp.asarray(0.125, bf)
        qkv_s[:, D:] = qkv[:, D:]
        gm_s[...] = mm(cw, wproj_ref[...]).astype(bf)
        win_row = win_ref[0:1, :] + (lat_shift - WROWS + WROWS * k)
        row_own = (win_row >= 0) & (win_row < ROWS)
        for m in range(MBLOCKS):
            if between is not None and m in between:
                between[m]()
            sl = slice(m * WPAD, m * WPAD + WPAD)
            key = key_s[k, sl, :]
            win_col = win_ref[1:2, :] + (lon_shift - WCOLS + WCOLS * m)
            own = jnp.where(row_own & (win_col >= 0) & (win_col < COLS), 1.0, 0.0)
            for q in range(2):
                lo = 256 * q
                qq = qkv_s[sl, lo : lo + 256]
                kq = qkv_s[sl, D + lo : D + lo + 256]
                vq = qkv_s[sl, 2 * D + lo : 2 * D + lo + 256]
                mq = gm_s[sl, lo : lo + 256]
                kst = jnp.concatenate([kq * h for h in head_masks], axis=0)
                vst = jnp.concatenate([vq * h for h in head_masks], axis=0)
                st = mm_nt(kst, qq).reshape(4, WPAD, WPAD)
                st = (st + bias_s[4 * q : 4 * q + 4]) + key[None]
                top = jnp.max(st, axis=1, keepdims=True)
                ex = jnp.exp(st - top)
                pr = ex * (1.0 / jnp.sum(ex, axis=1, keepdims=True))
                prh = pr.astype(bf).reshape(4 * WPAD, WPAD)
                gp = mm_nt(vst, mq).reshape(4, WPAD, WPAD)
                pg = pr * gp
                ds = pr * (gp - jnp.sum(pg, axis=1, keepdims=True))
                g_s[4 * q : 4 * q + 4] += ds * own[None]
                dsh = ds.astype(bf).reshape(4 * WPAD, WPAD)
                mix_s[sl, lo : lo + 256] = mm_tn(prh, vst).astype(bf)
                gc_s[sl, lo : lo + 256] = (mm_tn(dsh, kst) * 0.125).astype(bf)
                gk = mm(dsh, qq).reshape(4, WPAD, 256)
                gv = mm(prh, mq).reshape(4, WPAD, 256)
                for s, base in ((gk, D), (gv, 2 * D)):
                    for c in range(2):
                        lanes = slice(128 * c, 128 * c + 128)
                        both = jnp.where(half, s[2 * c, :, lanes], s[2 * c + 1, :, lanes])
                        gc_s[sl, base + lo + 128 * c : base + lo + 128 * c + 128] = both.astype(bf)
        rows = slice(WROWS * k, WROWS * k + WROWS)
        mixo_s[rows] = mm(put_s[...], mix_s[...]).astype(bf).reshape(WROWS, COLS, D)
        gco_s[rows] = mm(put_s[...], gc_s[...]).astype(bf).reshape(WROWS, COLS, 3 * D)

    side_cols = ((LEFT, slice(0, HALO_COLS)), (RIGHT, slice(HALO_COLS + COLS, EXT_COLS)))
    end_rows = ((UP, slice(0, HALO_ROWS)), (DOWN, slice(HALO_ROWS + ROWS, EXT_ROWS)))
    for copy in sides[0] + sides[1]:
        copy.wait()
    for s, cols in side_cols:
        norm = normalized(side_s[0, s].reshape(ROWS * HALO_COLS, D), gain)[2]
        norm_s[own_rows, cols] = norm.reshape(ROWS, HALO_COLS, D)
        cot_s[own_rows, cols] = side_s[1, s]
    strip(1, {2: lambda: pass_corners(0), 4: lambda: pass_corners(1)})
    for copy, there in corners[0] + corners[1]:
        pl.when(there)(copy.wait)
    for way, rows in end_rows:
        norm = normalized(vert_s[0, way].reshape(HALO_ROWS * EXT_COLS, D), gain)[2]
        norm_s[rows] = norm.reshape(HALO_ROWS, EXT_COLS, D)
        cot_s[rows] = vert_s[1, way]
    strip(0)
    strip(2)
    for i in range(2):
        for copy, sends, _ in vertical[i]:
            pl.when(sends)(copy.wait_send)

    cells = ROWS * COLS
    first = pl.ds(WROWS - lat_shift, ROWS)
    x = f_ref[...].reshape(cells, D).astype(f32)
    cot = c_ref[...].reshape(cells, D)
    norm = norm_s[own_rows, own_cols].reshape(cells, D)
    mean = mean_s[...]
    rstd = rstd_s[...]
    mixo = mixo_s[first].reshape(cells, D)
    gco = gco_s[first].reshape(cells, 3 * D)
    out_ref[...] = (x + mm_nt(mixo, wproj_ref[...])).astype(bf).reshape(ROWS, COLS, D)
    gn = mm(gco, wqkv_ref[...])
    xhat = (x - mean) * rstd
    gg = jnp.sum(gn * xhat, axis=0, keepdims=True)
    gs = gn * gain
    gin = rstd * (
        gs
        - jnp.mean(gs, axis=-1, keepdims=True)
        - xhat * jnp.mean(gs * xhat, axis=-1, keepdims=True)
    )
    gf_ref[...] = (cot.astype(f32) + gin).astype(bf).reshape(ROWS, COLS, D)
    gq = mm_tn(gco, norm).astype(bf)
    gp = mm_tn(cot, mixo).astype(bf)
    for o in range(32):
        rows = jnp.concatenate([gq[48 * o : 48 * o + 48], gp[16 * o : 16 * o + 16]], axis=0)
        part_ref[64 * o : 64 * o + 64] = mm(perm_ref[...], rows).astype(bf)

    small_ref[...] = jnp.zeros_like(small_ref)
    parts = three_parts(g_s[...].reshape(HEADS * WPAD, WPAD))
    z = mm_nt(parts[2].astype(bf), obase_ref[...]) + mm_nt(parts[1].astype(bf), obase_ref[...])
    z = z + mm_nt(parts[0].astype(bf), obase_ref[...])
    z_s[...] = z.reshape(HEADS, WPAD, 128)
    zero = jnp.zeros((HEADS, 128), f32)
    table = jnp.zeros((HEADS, FLAT), f32)
    for j in range(WCELLS):
        wide = jnp.concatenate([z_s[:, j, :], zero], axis=1)
        table = table + pltpu.roll(wide, OFFSETS[j], 1)
    small_ref[:, :FLAT] = table
    for i in range(4):
        small_ref[i : i + 1, FLAT:] = gg[:, 128 * i : 128 * i + 128]


def local(shift, fields, cotangent, mask, gain, w_qkv, w_proj, rel):
    info, lanes, win, perm, obase = cell_tables()
    vmem = pl.BlockSpec(memory_space=pltpu.VMEM)
    smem = pl.BlockSpec(memory_space=pltpu.SMEM)
    tile = jax.ShapeDtypeStruct((ROWS, COLS, D), jnp.bfloat16)
    bf = jnp.bfloat16
    f32 = jnp.float32
    vm = pltpu.VMEM
    dma = pltpu.SemaphoreType.DMA
    strip_rows = KBLOCKS * WROWS
    return pl.pallas_call(
        local_kernel,
        out_shape=(
            tile,
            tile,
            jax.ShapeDtypeStruct((2048, D), bf),
            jax.ShapeDtypeStruct((8, MAIN), f32),
        ),
        in_specs=[smem] + [vmem] * 12,
        out_specs=(vmem,) * 4,
        scratch_shapes=[
            vm((16, 128), f32),
            vm((3, 3, 16, 128), f32),
            vm((2, 2, HALO_ROWS, EXT_COLS, D), bf),
            vm((2, 2, ROWS, HALO_COLS, D), bf),
            vm((EXT_ROWS, EXT_COLS, D), bf),
            vm((EXT_ROWS, EXT_COLS, D), bf),
            vm((ROWS * COLS, 1), f32),
            vm((ROWS * COLS, 1), f32),
            vm((2 * WROWS - 1, HEADS, FLAT), f32),
            vm((WCELLS, 24, 128), f32),
            vm((HEADS, WPAD, WPAD), f32),
            vm((HEADS, WPAD, WPAD), f32),
            vm((HEADS, WPAD, 128), f32),
            vm((KBLOCKS, STRIP, WROWS * EXT_COLS), bf),
            vm((WROWS * COLS, STRIP), bf),
            vm((KBLOCKS, STRIP, 1), f32),
            vm((STRIP, 3 * D), bf),
            vm((STRIP, D), bf),
            vm((STRIP, D), bf),
            vm((STRIP, 3 * D), bf),
            vm((strip_rows, COLS, D), bf),
            vm((strip_rows, COLS, 3 * D), bf),
            dma((24,)),
            dma((24,)),
        ],
        compiler_params=pltpu.CompilerParams(
            collective_id=0, has_side_effects=True, vmem_limit_bytes=56 * MB
        ),
        name="window_attention",
    )(
        shift, fields, cotangent, mask, gain, w_qkv, w_proj, rel,
        jnp.asarray(info), jnp.asarray(lanes), jnp.asarray(win), jnp.asarray(perm), jnp.asarray(obase),
    )


PLANE = 16
ZED = 8


def as_pair(x):
    hi = x.astype(jnp.bfloat16).astype(jnp.float32)
    return jnp.concatenate([hi, x - hi], axis=0).astype(jnp.bfloat16)


def reduce_kernel(
    part_ref, small_ref, rows_ref, proj_ref, table_ref, gain_ref,
    own_a, got_a, small_a, buf_b, got_b, buf_c, got_c, buf_z, got_z, buf_y, got_y,
    load_a, send_a, recv_a, send_b, recv_b, send_c, recv_c, send_z, recv_z, send_y, recv_y,
):
    bf = jnp.bfloat16
    f32 = jnp.float32
    lon = lax.axis_index("lon")
    lat = lax.axis_index("lat")
    lev = lax.axis_index("lev")
    zed = lon // 2
    core = lax.rem(lon, 2)
    plane = lat * 2 + lev
    sibling = (zed * 2 + (1 - core), lat, lev)

    def in_plane(p):
        return (lon, p // 2, lax.rem(p, 2))

    def along_z(z):
        return (z * 2 + core, lat, lev)

    barrier = pltpu.get_barrier_semaphore()
    pl.semaphore_signal(barrier, inc=1, device_id=sibling, device_id_type=MESH)
    for d in range(1, PLANE):
        p = lax.rem(plane + d, PLANE)
        pl.semaphore_signal(barrier, inc=1, device_id=in_plane(p), device_id_type=MESH)
    for d in range(1, ZED):
        z = lax.rem(zed + d, ZED)
        pl.semaphore_signal(barrier, inc=1, device_id=along_z(z), device_id_type=MESH)

    def remote(src, dst, send, recv, to):
        return pltpu.make_async_remote_copy(
            src_ref=src, dst_ref=dst, send_sem=send, recv_sem=recv, device_id=to, device_id_type=MESH
        )

    chunks = []
    for c in range(4):
        rows = pl.ds(pl.multiple_of(32 * lax.rem(plane // 4 + c, 4), 32), 32)
        there = remote(part_ref.at[:, 1 - core, rows], got_a.at[:, rows], send_a.at[c], recv_a.at[c], sibling)
        here = pltpu.make_async_copy(part_ref.at[:, core, rows], own_a.at[:, rows], load_a.at[c])
        here.start()
        chunks.append((there, here, rows))
    pl.semaphore_wait(barrier, 1 + PLANE - 1 + ZED - 1)
    copy_s = remote(small_ref, small_a, send_a.at[4], recv_a.at[4], sibling)
    copy_s.start()
    for there, _, _ in chunks:
        there.start()
    copy_s.wait()
    pair = as_pair(small_ref[...] + small_a[...])
    for p in range(PLANE):
        buf_b[p, 64:80] = pair

    def to_plane(p):
        return remote(buf_b.at[p], got_b.at[plane], send_b.at[p], recv_b.at[plane], in_plane(p))

    for c, (there, here, rows) in enumerate(chunks):
        here.wait()
        there.wait()
        base = 4 * lax.rem(plane // 4 + c, 4)
        for z in range(0, ZED, 2):
            lo = own_a[z, rows].astype(f32) + got_a[z, rows].astype(f32)
            hi = own_a[z + 1, rows].astype(f32) + got_a[z + 1, rows].astype(f32)
            both = jnp.concatenate([lo.reshape(4, 8, D), hi.reshape(4, 8, D)], axis=1)
            buf_b[pl.ds(base, 4), 8 * z : 8 * z + 16] = both[:, :, :MAIN].astype(bf)
            buf_z[z, rows] = lo[:, MAIN:].astype(bf)
            buf_z[z + 1, rows] = hi[:, MAIN:].astype(bf)
        for e in range(4):
            p = base + lax.rem(plane + e, 4)

            @pl.when(p != plane)
            def _(p=p):
                to_plane(p).start()

    for d in range(1, ZED):
        z = lax.rem(zed + d, ZED)
        remote(buf_z.at[z], got_z.at[zed], send_z.at[z], recv_z.at[zed], along_z(z)).start()
    got_b[plane, 64:80] = pair
    last = buf_z[zed].astype(f32)
    for d in range(1, ZED):
        z = lax.rem(zed + d, ZED)
        remote(buf_z.at[z], got_z.at[z], send_z.at[z], recv_z.at[z], along_z(z)).wait()
        last = last + got_z[z].astype(f32)
    buf_y[...] = last.reshape(PLANE, 8, D - MAIN)

    def to_keeper(p):
        return remote(buf_y.at[p], got_y.at[plane], send_y.at[p], recv_y.at[plane], in_plane(p))

    for d in range(1, PLANE):
        to_keeper(lax.rem(plane + d, PLANE)).start()

    acc = buf_b[plane, 0:64].astype(f32)
    for d in range(1, PLANE):
        p = lax.rem(plane + d, PLANE)
        remote(buf_b.at[p], got_b.at[p], send_b.at[p], recv_b.at[p], in_plane(p)).wait()
        acc = acc + got_b[p, 0:64].astype(f32)
    total = jnp.zeros((16, MAIN), f32)
    for p in range(PLANE):
        total = total + got_b[p, 64:80].astype(f32)
    pair = as_pair(total[:8] + total[8:])

    blocks = [slice(128 * i, 128 * i + 128) for i in range(3)]
    for z in range(ZED):
        piece = acc[8 * z : 8 * z + 8]
        stack = [piece[:, b] for b in blocks] + [jnp.zeros((8, 128), f32)]
        buf_c[z, 0:32] = jnp.concatenate(stack, axis=0).astype(bf)
        for i, b in enumerate(blocks):
            buf_c[z, 32 + 16 * i : 48 + 16 * i] = pair[:, b]

    def along(z):
        return remote(buf_c.at[z], got_c.at[zed], send_c.at[z], recv_c.at[zed], along_z(z))

    for d in range(1, ZED):
        along(lax.rem(zed + d, ZED)).start()
    got_c[zed] = buf_c[zed]
    last = buf_y[plane]
    for d in range(1, PLANE):
        p = lax.rem(plane + d, PLANE)
        remote(buf_y.at[p], got_y.at[p], send_y.at[p], recv_y.at[p], in_plane(p)).wait()
        last = last + got_y[p]
    for d in range(1, ZED):
        z = lax.rem(zed + d, ZED)
        remote(buf_c.at[z], got_c.at[z], send_c.at[z], recv_c.at[z], along_z(z)).wait()
    total = got_c[0].astype(f32)
    for z in range(1, ZED):
        total = total + got_c[z].astype(f32)
    for i, b in enumerate(blocks):
        rows_ref[:, b] = total[8 * i : 8 * i + 6]
        proj_ref[:, b] = total[8 * i + 6 : 8 * i + 8]
    rows_ref[:, MAIN:] = last[0:6]
    proj_ref[:, MAIN:] = last[6:8]
    small = [total[32 + 16 * i : 40 + 16 * i] + total[40 + 16 * i : 48 + 16 * i] for i in range(3)]
    flat = jnp.concatenate(small[:2], axis=1)
    for u in range(2 * WROWS - 1):
        table_ref[u] = pltpu.roll(flat, (FLAT - (2 * WCOLS - 1) * u) % FLAT, 1)[:, : 2 * WCOLS - 1]
    for i in range(4):
        gain_ref[:, 128 * i : 128 * i + 128] = small[2][i : i + 1]


def reduce_all(part, small):
    vmem = pl.BlockSpec(memory_space=pltpu.VMEM)
    f32 = jnp.float32
    bf = jnp.bfloat16
    vm = pltpu.VMEM
    dma = pltpu.SemaphoreType.DMA
    return pl.pallas_call(
        reduce_kernel,
        out_shape=(
            jax.ShapeDtypeStruct((6, D), f32),
            jax.ShapeDtypeStruct((2, D), f32),
            jax.ShapeDtypeStruct((2 * WROWS - 1, HEADS, 2 * WCOLS - 1), f32),
            jax.ShapeDtypeStruct((1, D), f32),
        ),
        in_specs=[pl.BlockSpec(memory_space=pl.ANY), vmem],
        out_specs=(vmem,) * 4,
        scratch_shapes=[
            vm((ZED, 128, D), bf),
            vm((ZED, 128, D), bf),
            vm((8, MAIN), f32),
            vm((PLANE, 80, MAIN), bf),
            vm((PLANE, 80, MAIN), bf),
            vm((ZED, 80, 128), bf),
            vm((ZED, 80, 128), bf),
            vm((ZED, 128, D - MAIN), bf),
            vm((ZED, 128, D - MAIN), bf),
            vm((PLANE, 8, D - MAIN), f32),
            vm((PLANE, 8, D - MAIN), f32),
            dma((4,)),
            dma((5,)),
            dma((5,)),
            dma((PLANE,)),
            dma((PLANE,)),
            dma((ZED,)),
            dma((ZED,)),
            dma((ZED,)),
            dma((ZED,)),
            dma((PLANE,)),
            dma((PLANE,)),
        ],
        compiler_params=pltpu.CompilerParams(
            collective_id=1, has_side_effects=True, vmem_limit_bytes=60 * MB
        ),
        name="reduce_gradients",
    )(part.reshape(ZED, 2, 128, D), small)


def on_device(fields, cotangent, land_mask, shift_offsets, norm_gain, w_qkv, w_proj, rel_bias):
    rel = rel_bias.transpose(1, 0, 2)
    out, gf, part, small = local(
        shift_offsets, fields[0], cotangent[0], land_mask, norm_gain.reshape(1, D), w_qkv, w_proj, rel
    )
    rows, proj, table, ggain = reduce_all(part, small)
    return (out[None], gf[None], rows, proj, table.transpose(1, 0, 2), ggain.reshape(D))


def solution(mesh):
    return jax.shard_map(
        on_device,
        mesh=mesh,
        in_specs=(
            P("lev", "lat", "lon", None),
            P("lev", "lat", "lon", None),
            P("lat", "lon"),
            P(),
            P(),
            P(),
            P(),
            P(),
        ),
        out_specs=(
            P("lev", "lat", "lon", None),
            P("lev", "lat", "lon", None),
            P(("lon", "lat", "lev"), None),
            P(("lon", "lat", "lev"), None),
            P(),
            P(),
        ),
        check_vma=False,
    )
```

```python
import jax
import jax.numpy as jnp
import numpy as np
from jax import lax
from jax.experimental import pallas as pl
from jax.experimental.pallas import tpu as pltpu
from jax.sharding import PartitionSpec as P

MESH = pl.DeviceIdType.MESH
WROWS = 6
WCOLS = 12
WCELLS = WROWS * WCOLS
WPAD = 80
EPSILON = 1e-05
NEG_FILL = 100.0
D = 512
HEADS = 8
ROWS = 12
COLS = 48
HALO_ROWS = 5
HALO_COLS = 16
EXT_ROWS = ROWS + 2 * HALO_ROWS
EXT_COLS = COLS + 2 * HALO_COLS
KBLOCKS = ROWS // WROWS + 1
MBLOCKS = COLS // WCOLS + 1
STRIP = MBLOCKS * WPAD
LAT = 8
LON = 16
LEV = 2
MAIN = 384
MB = 1024 * 1024
NT = (((1,), (1,)), ((), ()))
TN = (((0,), (0,)), ((), ()))


def mm(a, b):
    return jnp.dot(a, b, preferred_element_type=jnp.float32)


def mm_nt(a, b):
    return lax.dot_general(a, b, NT, preferred_element_type=jnp.float32)


def mm_tn(a, b):
    return lax.dot_general(a, b, TN, preferred_element_type=jnp.float32)


UP, DOWN = 0, 1
LEFT, RIGHT = 0, 1
DIRECTIONS = [(dy, dx) for dy in (-1, 0, 1) for dx in (-1, 0, 1) if (dy, dx) != (0, 0)]
CENTRE = pl.ds(HALO_COLS, COLS)
FLAT = 256
OFFSETS = [(WROWS - 1) * (2 * WCOLS - 1) + WCOLS - 1 - (2 * WCOLS - 1) * (j // WCOLS) - j % WCOLS for j in range(WCELLS)]


def cell_tables():
    cell = np.arange(STRIP)
    m, t = cell // WPAD, cell % WPAD
    a, b = t // WCOLS, t % WCOLS
    real = t < WCELLS
    info = np.zeros((STRIP, 4), np.int32)
    info[:, 0] = np.where(real, a * EXT_COLS + WCOLS * m + b, -100000)
    info[:, 1] = np.where(real, a, -1000)
    info[:, 2] = np.where(real, WCOLS * m + b, -1000)
    info[:, 3] = real
    lanes = np.zeros((8, STRIP), np.int32)
    lanes[0] = np.where(real, a * COLS, -100000)
    lanes[1] = np.where(real, WCOLS * m + b, -100000)
    win = np.zeros((8, WPAD), np.int32)
    t = np.arange(WPAD)
    win[0] = np.where(t < WCELLS, t // WCOLS, -1000)
    win[1] = np.where(t < WCELLS, t % WCOLS, -1000)
    perm = np.zeros((64, 64), np.float32)
    for o in range(8):
        for r in range(6):
            perm[8 * o + r, 6 * o + r] = 1
        for r in range(2):
            perm[8 * o + 6 + r, 48 + 2 * o + r] = 1
    base = np.where(t < WCELLS, (2 * WCOLS - 1) * (t // WCOLS) + t % WCOLS, -1)
    obase = (np.arange(128)[:, None] == base[None, :]).astype(np.float32)
    return info, lanes, win, perm.astype(jnp.bfloat16), obase.astype(jnp.bfloat16)


def three_parts(x):
    hi = x.astype(jnp.bfloat16).astype(jnp.float32)
    rest = x - hi
    mid = rest.astype(jnp.bfloat16).astype(jnp.float32)
    return hi, mid, rest - mid


def normalized(x, gain):
    x = x.astype(jnp.float32)
    mean = jnp.mean(x, axis=-1, keepdims=True)
    cen = x - mean
    rstd = lax.rsqrt(jnp.mean(cen * cen, axis=-1, keepdims=True) + EPSILON)
    return mean, rstd, (cen * rstd * gain).astype(jnp.bfloat16)


def local_kernel(
    shift,
    f_ref,
    c_ref,
    m_ref,
    gain_ref,
    wqkv_ref,
    wproj_ref,
    rel_ref,
    info_ref,
    lanes_ref,
    win_ref,
    perm_ref,
    obase_ref,
    mixed_ref,
    gn_ref,
    part_ref,
    small_ref,
    tile_s,
    mx_s,
    vert_s,
    side_s,
    norm_s,
    cot_s,
    mean_s,
    rstd_s,
    rel_s,
    roll_s,
    bias_s,
    g_s,
    z_s,
    pick_s,
    put_s,
    key_s,
    qkv_s,
    gm_s,
    mix_s,
    gc_s,
    mixo_s,
    gco_s,
    send,
    recv,
):
    bf = jnp.bfloat16
    f32 = jnp.float32
    lon = lax.axis_index("lon")
    lat = lax.axis_index("lat")
    lev = lax.axis_index("lev")
    lat_shift = 1 + jnp.mod(shift[0], WROWS - 1)
    lon_shift = 1 + jnp.mod(shift[1], WCOLS - 1)
    lat_base = lat * ROWS
    has_above = lat > 0
    has_below = lat < LAT - 1
    true = lat >= 0

    def neighbour(dy, dx):
        return (lax.rem(lon + dx + LON, LON), lat + dy, lev)

    def exists(dy):
        return {-1: has_above, 0: true, 1: has_below}[dy]

    def remote(src, dst, n, to):
        return pltpu.make_async_remote_copy(
            src_ref=src, dst_ref=dst, send_sem=send.at[n], recv_sem=recv.at[n], device_id=to, device_id_type=MESH
        )

    barrier = pltpu.get_barrier_semaphore()
    for dy, dx in DIRECTIONS:

        @pl.when(exists(dy))
        def _(dy=dy, dx=dx):
            pl.semaphore_signal(barrier, inc=1, device_id=neighbour(dy, dx), device_id_type=MESH)

    tile_s[...] = jnp.zeros_like(tile_s)
    tile_s[:ROWS, :COLS] = m_ref[...].astype(f32)
    mx_s[1, 1] = tile_s[...]
    for absent, rows in ((lat == 0, UP), (lat == LAT - 1, DOWN)):

        @pl.when(absent)
        def _(rows=rows):
            vert_s[:, rows] = jnp.zeros_like(vert_s[:, rows])
            for block in range(3):
                mx_s[block, 2 * rows] = jnp.zeros((16, 128), f32)

    @pl.when(has_above & has_below)
    def _():
        pl.semaphore_wait(barrier, 8)

    @pl.when(~(has_above & has_below))
    def _():
        pl.semaphore_wait(barrier, 5)

    masks = []
    for n, (dy, dx) in enumerate(DIRECTIONS):
        copy = remote(tile_s, mx_s.at[1 - dx, 1 - dy], n, neighbour(dy, dx))
        masks.append((copy, exists(dy), exists(-dy)))
    vertical = [[], []]
    sides = [[], []]
    corners = [[], []]
    for i, src in enumerate((f_ref, c_ref)):
        for way, dy, rows in (
            (DOWN, -1, pl.ds(0, HALO_ROWS)),
            (UP, 1, pl.ds(ROWS - HALO_ROWS, HALO_ROWS)),
        ):
            copy = remote(src.at[rows], vert_s.at[i, way, :, CENTRE], 8 + 2 * way + i, neighbour(dy, 0))
            vertical[i].append((copy, exists(dy), exists(-dy)))
        for s, dx, cols in ((LEFT, 1, pl.ds(COLS - HALO_COLS, HALO_COLS)), (RIGHT, -1, pl.ds(0, HALO_COLS))):
            sides[i].append(remote(src.at[:, cols], side_s.at[i, s], 12 + 2 * s + i, neighbour(0, dx)))
        for way, there in ((UP, has_above), (DOWN, has_below)):
            for s, dx, cols, dst in (
                (LEFT, 1, pl.ds(COLS, HALO_COLS), pl.ds(0, HALO_COLS)),
                (RIGHT, -1, pl.ds(HALO_COLS, HALO_COLS), pl.ds(HALO_COLS + COLS, HALO_COLS)),
            ):
                n = 16 + 4 * way + 2 * s + i
                copy = remote(vert_s.at[i, way, :, cols], vert_s.at[i, way, :, dst], n, neighbour(0, dx))
                corners[i].append((copy, there))
    for copy, sends, _ in masks:
        pl.when(sends)(copy.start)
    for i in range(2):
        for copy, sends, _ in vertical[i]:
            pl.when(sends)(copy.start)
        for copy in sides[i]:
            copy.start()

    def pass_corners(i):
        for copy, _, receives in vertical[i]:
            pl.when(receives)(copy.wait_recv)
        for copy, there in corners[i]:
            pl.when(there)(copy.start)

    gain = gain_ref[...]
    half = lax.broadcasted_iota(jnp.int32, (1, 128), 1) < 64
    lane4 = lax.broadcasted_iota(jnp.int32, (1, 256), 1)
    head_masks = [
        jnp.where((lane4 >= 64 * h) & (lane4 < 64 * h + 64), 1.0, 0.0).astype(bf) for h in range(4)
    ]
    g_s[...] = jnp.zeros_like(g_s)

    mean, rstd, norm = normalized(f_ref[...].reshape(ROWS * COLS, D), gain)
    mean_s[...] = mean
    rstd_s[...] = rstd
    own_rows = slice(HALO_ROWS, HALO_ROWS + ROWS)
    own_cols = slice(HALO_COLS, HALO_COLS + COLS)
    norm_s[own_rows, own_cols] = norm.reshape(ROWS, COLS, D)
    cot_s[own_rows, own_cols] = c_ref[...]

    rel_s[...] = jnp.zeros_like(rel_s)
    flat = jnp.zeros((HEADS, FLAT), f32)
    for u in range(2 * WROWS - 1):
        rel_s[u, :, : 2 * WCOLS - 1] = rel_ref[u]
        flat = flat + pltpu.roll(rel_s[u], (2 * WCOLS - 1) * u, 1)
    rel3 = jnp.concatenate(three_parts(flat), axis=0)
    for j in range(WCELLS):
        roll_s[j] = pltpu.roll(rel3, (FLAT - OFFSETS[j]) % FLAT, 1)[:, :128]
    pairs = mm(roll_s[...].reshape(WCELLS * 24, 128).astype(bf), obase_ref[...])
    pairs = pairs.reshape(WCELLS, 24, WPAD)
    pairs = (pairs[:, 16:24] + pairs[:, 8:16]) + pairs[:, :8]
    bias_s[...] = jnp.zeros_like(bias_s)
    for j in range(WCELLS):
        bias_s[:, j, :] = pairs[j]

    acol = info_ref[:, 1:2]
    valid = []
    for k in range(KBLOCKS):
        grow = acol + (lat_shift - WROWS + WROWS * k + lat_base)
        valid.append((grow >= 0) & (grow < LAT * ROWS))
        target = jnp.where(valid[k], info_ref[:, 0:1] + (lon_shift + 4), -1)
        lane = lax.broadcasted_iota(jnp.int32, (STRIP, WROWS * EXT_COLS), 1)
        pick_s[k] = jnp.where(lane == target, 1.0, 0.0).astype(bf)
    xl = lanes_ref[1:2, :] + (lon_shift - WCOLS)
    place = jnp.where((xl >= 0) & (xl < COLS), lanes_ref[0:1, :] + xl, -1)
    sub = lax.broadcasted_iota(jnp.int32, (WROWS * COLS, STRIP), 0)
    put_s[...] = jnp.where(sub == place, 1.0, 0.0).astype(bf)

    for copy, sends, receives in masks:
        pl.when(sends)(copy.wait_send)
        pl.when(receives)(copy.wait_recv)
    xcol = info_ref[:, 2:3] + (lon_shift + 4)
    lane = lax.broadcasted_iota(jnp.int32, (STRIP, 128), 1)
    by_row = 0.0
    for block, offset in enumerate((32, -16, -64)):
        mpick = jnp.where(lane == xcol + offset, 1.0, 0.0).astype(bf)
        by_row = by_row + mm_nt(mpick, mx_s[block].reshape(48, 128).astype(bf))
    lane = lax.broadcasted_iota(jnp.int32, (STRIP, 48), 1)
    for k in range(KBLOCKS):
        erow = acol + (lat_shift - 1 + WROWS * k)
        flat = jnp.where(erow < 5, erow + 7, jnp.where(erow < 17, erow + 11, erow + 15))
        keep = jnp.sum(jnp.where((lane == flat) & valid[k], by_row, 0.0), axis=-1, keepdims=True)
        key_s[k] = jnp.where(info_ref[:, 3:4] > 0, NEG_FILL * (keep - 1.0), -1e30)

    def rows_of(k):
        return pl.ds(lat_shift - 1 + WROWS * k, WROWS)

    def strip(k, between=None):
        norm = norm_s[rows_of(k)].reshape(WROWS * EXT_COLS, D)
        cot = cot_s[rows_of(k)].reshape(WROWS * EXT_COLS, D)
        nw = mm(pick_s[k], norm).astype(bf)
        cw = mm(pick_s[k], cot).astype(bf)
        qkv = mm_nt(nw, wqkv_ref[...]).astype(bf)
        qkv_s[:, :D] = qkv[:, :D] * jnp.asarray(0.125, bf)
        qkv_s[:, D:] = qkv[:, D:]
        gm_s[...] = mm(cw, wproj_ref[...]).astype(bf)
        win_row = win_ref[0:1, :] + (lat_shift - WROWS + WROWS * k)
        row_own = (win_row >= 0) & (win_row < ROWS)
        for m in range(MBLOCKS):
            if between is not None and m in between:
                between[m]()
            sl = slice(m * WPAD, m * WPAD + WPAD)
            key = key_s[k, sl, :]
            win_col = win_ref[1:2, :] + (lon_shift - WCOLS + WCOLS * m)
            own = jnp.where(row_own & (win_col >= 0) & (win_col < COLS), 1.0, 0.0)
            for q in range(2):
                lo = 256 * q
                qq = qkv_s[sl, lo : lo + 256]
                kq = qkv_s[sl, D + lo : D + lo + 256]
                vq = qkv_s[sl, 2 * D + lo : 2 * D + lo + 256]
                mq = gm_s[sl, lo : lo + 256]
                kst = jnp.concatenate([kq * h for h in head_masks], axis=0)
                vst = jnp.concatenate([vq * h for h in head_masks], axis=0)
                st = mm_nt(kst, qq).reshape(4, WPAD, WPAD)
                st = (st + bias_s[4 * q : 4 * q + 4]) + key[None]
                top = jnp.max(st, axis=1, keepdims=True)
                ex = jnp.exp(st - top)
                pr = ex * (1.0 / jnp.sum(ex, axis=1, keepdims=True))
                prh = pr.astype(bf).reshape(4 * WPAD, WPAD)
                gp = mm_nt(vst, mq).reshape(4, WPAD, WPAD)
                pg = pr * gp
                ds = pr * (gp - jnp.sum(pg, axis=1, keepdims=True))
                g_s[4 * q : 4 * q + 4] += ds * own[None]
                dsh = ds.astype(bf).reshape(4 * WPAD, WPAD)
                mix_s[sl, lo : lo + 256] = mm_tn(prh, vst).astype(bf)
                gc_s[sl, lo : lo + 256] = (mm_tn(dsh, kst) * 0.125).astype(bf)
                gk = mm(dsh, qq).reshape(4, WPAD, 256)
                gv = mm(prh, mq).reshape(4, WPAD, 256)
                for s, base in ((gk, D), (gv, 2 * D)):
                    for c in range(2):
                        lanes = slice(128 * c, 128 * c + 128)
                        both = jnp.where(half, s[2 * c, :, lanes], s[2 * c + 1, :, lanes])
                        gc_s[sl, base + lo + 128 * c : base + lo + 128 * c + 128] = both.astype(bf)
        rows = slice(WROWS * k, WROWS * k + WROWS)
        mixo_s[rows] = mm(put_s[...], mix_s[...]).astype(bf).reshape(WROWS, COLS, D)
        gco_s[rows] = mm(put_s[...], gc_s[...]).astype(bf).reshape(WROWS, COLS, 3 * D)

    side_cols = ((LEFT, slice(0, HALO_COLS)), (RIGHT, slice(HALO_COLS + COLS, EXT_COLS)))
    end_rows = ((UP, slice(0, HALO_ROWS)), (DOWN, slice(HALO_ROWS + ROWS, EXT_ROWS)))
    for copy in sides[0] + sides[1]:
        copy.wait()
    for s, cols in side_cols:
        norm = normalized(side_s[0, s].reshape(ROWS * HALO_COLS, D), gain)[2]
        norm_s[own_rows, cols] = norm.reshape(ROWS, HALO_COLS, D)
        cot_s[own_rows, cols] = side_s[1, s]
    strip(1, {2: lambda: pass_corners(0), 4: lambda: pass_corners(1)})
    for copy, there in corners[0] + corners[1]:
        pl.when(there)(copy.wait)
    for way, rows in end_rows:
        norm = normalized(vert_s[0, way].reshape(HALO_ROWS * EXT_COLS, D), gain)[2]
        norm_s[rows] = norm.reshape(HALO_ROWS, EXT_COLS, D)
        cot_s[rows] = vert_s[1, way]
    strip(0)
    strip(2)
    for i in range(2):
        for copy, sends, _ in vertical[i]:
            pl.when(sends)(copy.wait_send)

    cells = ROWS * COLS
    first = pl.ds(WROWS - lat_shift, ROWS)
    x = f_ref[...].reshape(cells, D).astype(f32)
    cot = c_ref[...].reshape(cells, D)
    norm = norm_s[own_rows, own_cols].reshape(cells, D)
    mean = mean_s[...]
    rstd = rstd_s[...]
    mixo = mixo_s[first].reshape(cells, D)
    gco = gco_s[first].reshape(cells, 3 * D)
    mixed_ref[...] = mixo
    gn = mm(gco, wqkv_ref[...])
    gn_ref[...] = gn
    xhat = (x - mean) * rstd
    gg = jnp.sum(gn * xhat, axis=0, keepdims=True)
    gq = mm_tn(gco, norm).astype(bf)
    gp = mm_tn(cot, mixo).astype(bf)
    for o in range(32):
        rows = jnp.concatenate([gq[48 * o : 48 * o + 48], gp[16 * o : 16 * o + 16]], axis=0)
        part_ref[64 * o : 64 * o + 64] = mm(perm_ref[...], rows).astype(bf)

    small_ref[...] = jnp.zeros_like(small_ref)
    parts = three_parts(g_s[...].reshape(HEADS * WPAD, WPAD))
    z = mm_nt(parts[2].astype(bf), obase_ref[...]) + mm_nt(parts[1].astype(bf), obase_ref[...])
    z = z + mm_nt(parts[0].astype(bf), obase_ref[...])
    z_s[...] = z.reshape(HEADS, WPAD, 128)
    zero = jnp.zeros((HEADS, 128), f32)
    table = jnp.zeros((HEADS, FLAT), f32)
    for j in range(WCELLS):
        wide = jnp.concatenate([z_s[:, j, :], zero], axis=1)
        table = table + pltpu.roll(wide, OFFSETS[j], 1)
    small_ref[:, :FLAT] = table
    for i in range(4):
        small_ref[i : i + 1, FLAT:] = gg[:, 128 * i : 128 * i + 128]


def local(shift, fields, cotangent, mask, gain, w_qkv, w_proj, rel):
    info, lanes, win, perm, obase = cell_tables()
    vmem = pl.BlockSpec(memory_space=pltpu.VMEM)
    smem = pl.BlockSpec(memory_space=pltpu.SMEM)
    bf = jnp.bfloat16
    f32 = jnp.float32
    vm = pltpu.VMEM
    dma = pltpu.SemaphoreType.DMA
    strip_rows = KBLOCKS * WROWS
    return pl.pallas_call(
        local_kernel,
        out_shape=(
            jax.ShapeDtypeStruct((ROWS * COLS, D), bf),
            jax.ShapeDtypeStruct((ROWS * COLS, D), f32),
            jax.ShapeDtypeStruct((2048, D), bf),
            jax.ShapeDtypeStruct((8, MAIN), f32),
        ),
        in_specs=[smem] + [vmem] * 12,
        out_specs=(vmem,) * 4,
        scratch_shapes=[
            vm((16, 128), f32),
            vm((3, 3, 16, 128), f32),
            vm((2, 2, HALO_ROWS, EXT_COLS, D), bf),
            vm((2, 2, ROWS, HALO_COLS, D), bf),
            vm((EXT_ROWS, EXT_COLS, D), bf),
            vm((EXT_ROWS, EXT_COLS, D), bf),
            vm((ROWS * COLS, 1), f32),
            vm((ROWS * COLS, 1), f32),
            vm((2 * WROWS - 1, HEADS, FLAT), f32),
            vm((WCELLS, 24, 128), f32),
            vm((HEADS, WPAD, WPAD), f32),
            vm((HEADS, WPAD, WPAD), f32),
            vm((HEADS, WPAD, 128), f32),
            vm((KBLOCKS, STRIP, WROWS * EXT_COLS), bf),
            vm((WROWS * COLS, STRIP), bf),
            vm((KBLOCKS, STRIP, 1), f32),
            vm((STRIP, 3 * D), bf),
            vm((STRIP, D), bf),
            vm((STRIP, D), bf),
            vm((STRIP, 3 * D), bf),
            vm((strip_rows, COLS, D), bf),
            vm((strip_rows, COLS, 3 * D), bf),
            dma((24,)),
            dma((24,)),
        ],
        compiler_params=pltpu.CompilerParams(
            collective_id=0, has_side_effects=True, vmem_limit_bytes=56 * MB
        ),
        name="window_attention",
    )(
        shift, fields, cotangent, mask, gain, w_qkv, w_proj, rel,
        jnp.asarray(info), jnp.asarray(lanes), jnp.asarray(win), jnp.asarray(perm), jnp.asarray(obase),
    )


PLANE = 16
ZED = 8


def as_pair(x):
    hi = x.astype(jnp.bfloat16).astype(jnp.float32)
    return jnp.concatenate([hi, x - hi], axis=0).astype(jnp.bfloat16)


def reduce_kernel(
    part_ref, small_ref, f_ref, c_ref, mixed_ref, gn_ref, wproj_ref, norm_gain_ref,
    rows_ref, proj_ref, table_ref, gain_ref, out_ref, gf_ref, f_s, c_s, mixed_s, gn_s, wproj_s,
    own_a, got_a, small_a, buf_b, got_b, buf_c, got_c, buf_z, got_z, buf_y, got_y,
    load, load_a, send_a, recv_a, send_b, recv_b, send_c, recv_c, send_z, recv_z, send_y, recv_y,
):
    bf = jnp.bfloat16
    f32 = jnp.float32
    lon = lax.axis_index("lon")
    lat = lax.axis_index("lat")
    lev = lax.axis_index("lev")
    zed = lon // 2
    core = lax.rem(lon, 2)
    plane = lat * 2 + lev
    sibling = (zed * 2 + (1 - core), lat, lev)

    def in_plane(p):
        return (lon, p // 2, lax.rem(p, 2))

    def along_z(z):
        return (z * 2 + core, lat, lev)

    barrier = pltpu.get_barrier_semaphore()
    pl.semaphore_signal(barrier, inc=1, device_id=sibling, device_id_type=MESH)
    for d in range(1, PLANE):
        p = lax.rem(plane + d, PLANE)
        pl.semaphore_signal(barrier, inc=1, device_id=in_plane(p), device_id_type=MESH)
    for d in range(1, ZED):
        z = lax.rem(zed + d, ZED)
        pl.semaphore_signal(barrier, inc=1, device_id=along_z(z), device_id_type=MESH)

    def remote(src, dst, send, recv, to):
        return pltpu.make_async_remote_copy(
            src_ref=src, dst_ref=dst, send_sem=send, recv_sem=recv, device_id=to, device_id_type=MESH
        )

    chunks = []
    for c in range(4):
        rows = pl.ds(pl.multiple_of(32 * lax.rem(plane // 4 + c, 4), 32), 32)
        there = remote(part_ref.at[:, 1 - core, rows], got_a.at[:, rows], send_a.at[c], recv_a.at[c], sibling)
        here = pltpu.make_async_copy(part_ref.at[:, core, rows], own_a.at[:, rows], load_a.at[c])
        here.start()
        chunks.append((there, here, rows))
    loads = [
        pltpu.make_async_copy(src, dst, load.at[i])
        for i, (src, dst) in enumerate(
            ((f_ref, f_s), (c_ref, c_s), (mixed_ref, mixed_s), (gn_ref, gn_s), (wproj_ref, wproj_s))
        )
    ]
    for copy in loads:
        copy.start()
    pl.semaphore_wait(barrier, 1 + PLANE - 1 + ZED - 1)
    copy_s = remote(small_ref, small_a, send_a.at[4], recv_a.at[4], sibling)
    copy_s.start()
    for there, _, _ in chunks:
        there.start()
    copy_s.wait()
    pair = as_pair(small_ref[...] + small_a[...])
    for p in range(PLANE):
        buf_b[p, 64:80] = pair

    def to_plane(p):
        return remote(buf_b.at[p], got_b.at[plane], send_b.at[p], recv_b.at[plane], in_plane(p))

    for c, (there, here, rows) in enumerate(chunks):
        here.wait()
        there.wait()
        base = 4 * lax.rem(plane // 4 + c, 4)
        for z in range(0, ZED, 2):
            lo = own_a[z, rows].astype(f32) + got_a[z, rows].astype(f32)
            hi = own_a[z + 1, rows].astype(f32) + got_a[z + 1, rows].astype(f32)
            both = jnp.concatenate([lo.reshape(4, 8, D), hi.reshape(4, 8, D)], axis=1)
            buf_b[pl.ds(base, 4), 8 * z : 8 * z + 16] = both[:, :, :MAIN].astype(bf)
            buf_z[z, rows] = lo[:, MAIN:].astype(bf)
            buf_z[z + 1, rows] = hi[:, MAIN:].astype(bf)
        for e in range(4):
            p = base + lax.rem(plane + e, 4)

            @pl.when(p != plane)
            def _(p=p):
                to_plane(p).start()

    for d in range(1, ZED):
        z = lax.rem(zed + d, ZED)
        remote(buf_z.at[z], got_z.at[zed], send_z.at[z], recv_z.at[zed], along_z(z)).start()
    got_b[plane, 64:80] = pair
    for copy in loads:
        copy.wait()
    x = f_s[...].reshape(ROWS * COLS, D).astype(f32)
    out_ref[...] = (x + mm_nt(mixed_s[...], wproj_s[...])).astype(bf).reshape(ROWS, COLS, D)
    cen = x - jnp.mean(x, axis=-1, keepdims=True)
    rstd = lax.rsqrt(jnp.mean(cen * cen, axis=-1, keepdims=True) + EPSILON)
    xhat = cen * rstd
    gs = gn_s[...] * norm_gain_ref[...]
    gin = rstd * (
        gs
        - jnp.mean(gs, axis=-1, keepdims=True)
        - xhat * jnp.mean(gs * xhat, axis=-1, keepdims=True)
    )
    cot = c_s[...].reshape(ROWS * COLS, D).astype(f32)
    gf_ref[...] = (cot + gin).astype(bf).reshape(ROWS, COLS, D)
    last = buf_z[zed].astype(f32)
    for d in range(1, ZED):
        z = lax.rem(zed + d, ZED)
        remote(buf_z.at[z], got_z.at[z], send_z.at[z], recv_z.at[z], along_z(z)).wait()
        last = last + got_z[z].astype(f32)
    buf_y[...] = last.reshape(PLANE, 8, D - MAIN)

    def to_keeper(p):
        return remote(buf_y.at[p], got_y.at[plane], send_y.at[p], recv_y.at[plane], in_plane(p))

    for d in range(1, PLANE):
        to_keeper(lax.rem(plane + d, PLANE)).start()

    acc = buf_b[plane, 0:64].astype(f32)
    for d in range(1, PLANE):
        p = lax.rem(plane + d, PLANE)
        remote(buf_b.at[p], got_b.at[p], send_b.at[p], recv_b.at[p], in_plane(p)).wait()
        acc = acc + got_b[p, 0:64].astype(f32)
    total = jnp.zeros((16, MAIN), f32)
    for p in range(PLANE):
        total = total + got_b[p, 64:80].astype(f32)
    pair = as_pair(total[:8] + total[8:])

    blocks = [slice(128 * i, 128 * i + 128) for i in range(3)]
    for z in range(ZED):
        piece = acc[8 * z : 8 * z + 8]
        stack = [piece[:, b] for b in blocks] + [jnp.zeros((8, 128), f32)]
        buf_c[z, 0:32] = jnp.concatenate(stack, axis=0).astype(bf)
        for i, b in enumerate(blocks):
            buf_c[z, 32 + 16 * i : 48 + 16 * i] = pair[:, b]

    def along(z):
        return remote(buf_c.at[z], got_c.at[zed], send_c.at[z], recv_c.at[zed], along_z(z))

    for d in range(1, ZED):
        along(lax.rem(zed + d, ZED)).start()
    got_c[zed] = buf_c[zed]
    last = buf_y[plane]
    for d in range(1, PLANE):
        p = lax.rem(plane + d, PLANE)
        remote(buf_y.at[p], got_y.at[p], send_y.at[p], recv_y.at[p], in_plane(p)).wait()
        last = last + got_y[p]
    for d in range(1, ZED):
        z = lax.rem(zed + d, ZED)
        remote(buf_c.at[z], got_c.at[z], send_c.at[z], recv_c.at[z], along_z(z)).wait()
    total = got_c[0].astype(f32)
    for z in range(1, ZED):
        total = total + got_c[z].astype(f32)
    for i, b in enumerate(blocks):
        rows_ref[:, b] = total[8 * i : 8 * i + 6]
        proj_ref[:, b] = total[8 * i + 6 : 8 * i + 8]
    rows_ref[:, MAIN:] = last[0:6]
    proj_ref[:, MAIN:] = last[6:8]
    small = [total[32 + 16 * i : 40 + 16 * i] + total[40 + 16 * i : 48 + 16 * i] for i in range(3)]
    flat = jnp.concatenate(small[:2], axis=1)
    for u in range(2 * WROWS - 1):
        table_ref[u] = pltpu.roll(flat, (FLAT - (2 * WCOLS - 1) * u) % FLAT, 1)[:, : 2 * WCOLS - 1]
    for i in range(4):
        gain_ref[:, 128 * i : 128 * i + 128] = small[2][i : i + 1]


def reduce_all(part, small, fields, cotangent, mixed, gn, w_proj, gain):
    vmem = pl.BlockSpec(memory_space=pltpu.VMEM)
    hbm = pl.BlockSpec(memory_space=pl.ANY)
    f32 = jnp.float32
    bf = jnp.bfloat16
    vm = pltpu.VMEM
    dma = pltpu.SemaphoreType.DMA
    return pl.pallas_call(
        reduce_kernel,
        out_shape=(
            jax.ShapeDtypeStruct((6, D), f32),
            jax.ShapeDtypeStruct((2, D), f32),
            jax.ShapeDtypeStruct((2 * WROWS - 1, HEADS, 2 * WCOLS - 1), f32),
            jax.ShapeDtypeStruct((1, D), f32),
            jax.ShapeDtypeStruct((ROWS, COLS, D), bf),
            jax.ShapeDtypeStruct((ROWS, COLS, D), bf),
        ),
        in_specs=[hbm, vmem, hbm, hbm, hbm, hbm, hbm, vmem],
        out_specs=(vmem,) * 6,
        scratch_shapes=[
            vm((ROWS, COLS, D), bf),
            vm((ROWS, COLS, D), bf),
            vm((ROWS * COLS, D), bf),
            vm((ROWS * COLS, D), f32),
            vm((D, D), bf),
            vm((ZED, 128, D), bf),
            vm((ZED, 128, D), bf),
            vm((8, MAIN), f32),
            vm((PLANE, 80, MAIN), bf),
            vm((PLANE, 80, MAIN), bf),
            vm((ZED, 80, 128), bf),
            vm((ZED, 80, 128), bf),
            vm((ZED, 128, D - MAIN), bf),
            vm((ZED, 128, D - MAIN), bf),
            vm((PLANE, 8, D - MAIN), f32),
            vm((PLANE, 8, D - MAIN), f32),
            dma((5,)),
            dma((4,)),
            dma((5,)),
            dma((5,)),
            dma((PLANE,)),
            dma((PLANE,)),
            dma((ZED,)),
            dma((ZED,)),
            dma((ZED,)),
            dma((ZED,)),
            dma((PLANE,)),
            dma((PLANE,)),
        ],
        compiler_params=pltpu.CompilerParams(
            collective_id=1, has_side_effects=True, vmem_limit_bytes=60 * MB
        ),
        name="reduce_gradients",
    )(part.reshape(ZED, 2, 128, D), small, fields, cotangent, mixed, gn, w_proj, gain)


def on_device(fields, cotangent, land_mask, shift_offsets, norm_gain, w_qkv, w_proj, rel_bias):
    rel = rel_bias.transpose(1, 0, 2)
    gain = norm_gain.reshape(1, D)
    mixed, gn, part, small = local(
        shift_offsets, fields[0], cotangent[0], land_mask, gain, w_qkv, w_proj, rel
    )
    rows, proj, table, ggain, out, gf = reduce_all(
        part, small, fields[0], cotangent[0], mixed, gn, w_proj, gain
    )
    return (out[None], gf[None], rows, proj, table.transpose(1, 0, 2), ggain.reshape(D))


def solution(mesh):
    return jax.shard_map(
        on_device,
        mesh=mesh,
        in_specs=(
            P("lev", "lat", "lon", None),
            P("lev", "lat", "lon", None),
            P("lat", "lon"),
            P(),
            P(),
            P(),
            P(),
            P(),
        ),
        out_specs=(
            P("lev", "lat", "lon", None),
            P("lev", "lat", "lon", None),
            P(("lon", "lat", "lev"), None),
            P(("lon", "lat", "lev"), None),
            P(),
            P(),
        ),
        check_vma=False,
    )
```
